32 devices in a mesh: px: 8 (over z, y), py: 4 (over x, core).
Axes of the slice: x: 2, y: 2, z: 4, core: 2. Of those that a mesh axis runs over, the one named last changes fastest.
Arguments:
- estimate: float32 [512, 512, 128], P('px', 'py'), may hold values from 0.2 to 5
- observed: float32 [512, 512, 128], P('px', 'py'), may hold values from 0.2 to 5
- psf: float32 [32, 32, 32], replicated, as said below
Outputs:
- updated: float32 [512, 512, 128], P('px', 'py')
The draws below stay inside these ranges and needn't reach their ends.
Inputs may be any that keep to these rules, and one draw needn't show every extreme that they name: `psf`: every entry is positive.
All inputs are finite; a program needn't handle non-finite values.
Results may differ from the reference program's by a relative error of at most 0.00009.
Values sent between devices are 32-bit elements; how exact they have to be, the bound alone decides.
A program may use at most 192 MiB of HBM per device.

```python
import math
import jax
import jax.numpy as jnp
from jax import lax

NX = 512
NY = 512
NZ = 128
P_SIZE = 32


def draw_psf(key, part):
    offsets = (jnp.arange(P_SIZE) - P_SIZE // 2).astype(jnp.float32)
    lateral = offsets[:, None, None] * offsets[:, None, None] + offsets[None, :, None] * offsets[None, :, None]
    axial = offsets[None, None, :] * offsets[None, None, :]
    radius = jnp.sqrt(lateral / 4.0 + axial / 16.0)
    factor = jnp.exp(jax.random.uniform(key, (P_SIZE, P_SIZE, P_SIZE), jnp.float32, math.log(0.5), math.log(2.0)))
    return factor * jnp.exp(-radius)


def levels(rng, dims, cuts, low, top_value):
    factor_of, own = 1.0, jax.random.fold_in(rng, 6)
    for dim, parts in cuts:
        draws = jnp.exp(jax.random.uniform(jax.random.fold_in(own, dim), (parts,), jnp.float32, low / len(cuts), top_value / len(cuts)))
        factor_of = factor_of * jnp.repeat(draws, dims[dim] // parts).reshape([-1 if axis == dim else 1 for axis in range(len(dims))])
    return factor_of


def setup_inputs(seed: int = 0) -> dict:
    key_of = jax.random.split(jax.random.key(seed), 4)
    return {
        "estimate": jnp.clip(jnp.exp(math.log(5.0) - 3.218876 * jax.random.uniform(key_of[0], (NX, NY, NZ), jnp.float32) ** levels(key_of[0], (NX, NY, NZ), ((0, 8), (1, 4)), -0.2, 0.2)), 0.2, 5.0),
        "observed": jnp.clip(jnp.exp(math.log(5.0) - 3.218876 * jax.random.uniform(key_of[1], (NX, NY, NZ), jnp.float32) ** levels(key_of[1], (NX, NY, NZ), ((0, 8), (1, 4)), -0.2, 0.2)), 0.2, 5.0),
        "psf": draw_psf(jax.random.fold_in(key_of[3], 71), 0),
    }


penalty_weight = 0.1
smoothing = 0.1

def backward_rows(flux):
    return flux - jnp.concatenate([jnp.zeros_like(flux[:1]), flux[:-1]], 0)

def backward_columns(flux):
    return flux - jnp.concatenate([jnp.zeros_like(flux[:, :1]), flux[:, :-1]], 1)

def backward_depth(flux):
    return flux - jnp.concatenate([jnp.zeros_like(flux[:, :, :1]), flux[:, :, :-1]], 2)

def variation(volume):
    slope_rows = jnp.concatenate([volume[1:] - volume[:-1], jnp.zeros_like(volume[:1])], 0)
    slope_cols = jnp.concatenate([volume[:, 1:] - volume[:, :-1], jnp.zeros_like(volume[:, :1])], 1)
    slope_depth = jnp.concatenate([volume[:, :, 1:] - volume[:, :, :-1], jnp.zeros_like(volume[:, :, :1])], 2)
    factor = lax.rsqrt(slope_rows * slope_rows + slope_cols * slope_cols + slope_depth * slope_depth + smoothing * smoothing)
    return backward_rows(slope_rows * factor) + backward_columns(slope_cols * factor) + backward_depth(slope_depth * factor)

def reference(estimate, observed, psf):
    padded = jnp.zeros((NX, NY, NZ), jnp.float32).at[:P_SIZE, :P_SIZE, :P_SIZE].set(psf)
    padded = jnp.roll(padded, (-(P_SIZE // 2), -(P_SIZE // 2), -(P_SIZE // 2)), axis=(0, 1, 2))
    transfer = jnp.fft.fftn(padded)
    blurred = jnp.real(jnp.fft.ifftn(jnp.fft.fftn(estimate) * transfer)).astype(jnp.float32)
    quotient = observed / blurred
    correction = jnp.real(jnp.fft.ifftn(jnp.fft.fftn(quotient) * jnp.conj(transfer))).astype(jnp.float32)
    divergence = variation(estimate)
    return estimate * correction / (1.0 - penalty_weight * divergence)
```

```python
import functools
import math

import jax
import jax.numpy as jnp
import ml_dtypes
import numpy as np
from jax import lax
from jax.experimental import pallas as pl
from jax.experimental.pallas import tpu as pltpu
from jax.sharding import PartitionSpec as P

penalty_weight = 0.1
smoothing = 0.1

LANES = 128
ROWS = 8
VMEM_LIMIT = 48 * 1024 * 1024


def halves(table):
    table = np.asarray(table, np.float64).astype(np.float32)
    high = table.astype(ml_dtypes.bfloat16)
    low = (table - high.astype(np.float32)).astype(ml_dtypes.bfloat16)
    return np.stack([high, low])


def waves(left, right, length):
    turns = np.remainder(np.outer(left, right), length) * (2.0 * math.pi / length)
    return np.cos(turns), np.sin(turns)


def up16(count):
    return -(-count // 16) * 16


def split(value):
    high = value.astype(jnp.bfloat16)
    low = (value - high.astype(jnp.float32)).astype(jnp.bfloat16)
    return high, low


def dot(left, right, dims):
    return lax.dot_general(left, right, (dims, ((), ())), preferred_element_type=jnp.float32)


def by_table(value, table, dims=((1,), (0,))):
    high, low = split(value)
    return dot(high, table[0], dims) + (dot(low, table[0], dims) + dot(high, table[1], dims))


def table_by(table, value, dims=((1,), (0,))):
    high, low = split(value)
    return dot(table[0], high, dims) + (dot(table[0], low, dims) + dot(table[1], high, dims))


class Plan:
    def __init__(self, rows, cols, depth, edge):
        half = edge // 2
        self.rows, self.cols, self.depth, self.edge, self.half = rows, cols, depth, edge, half
        self.row_whole = rows + edge
        self.col_whole = cols + edge
        self.modes = depth // 2 + 1
        self.mode_pad = up16(self.modes)
        modes = np.arange(self.modes)

        cosine, sine = waves(modes, np.arange(depth), depth)
        table = np.zeros((2 * self.mode_pad, depth))
        table[: self.modes] = cosine
        table[self.mode_pad : self.mode_pad + self.modes] = -sine
        self.depth_out = halves(table)
        weight = np.where((modes == 0) | (2 * modes == depth), 1.0, 2.0)
        weight = weight / (depth * self.row_whole * self.col_whole)
        table = np.zeros((self.mode_pad, 2 * depth))
        table[: self.modes, :depth] = cosine * weight[:, None]
        table[: self.modes, depth:] = -sine * weight[:, None]
        self.depth_home = halves(table)

        freq = np.arange(self.row_whole)
        place = np.concatenate([np.arange(rows + half), np.arange(-half, 0)])
        cosine, sine = waves(place, freq, self.row_whole)
        self.rows_out = halves(self.lane_table(cosine, -sine, LANES, LANES))
        cosine, sine = waves(freq, np.arange(rows), self.row_whole)
        self.rows_home = halves(self.lane_table(cosine, sine, LANES, rows))
        offset = np.arange(edge) - half
        cosine, sine = waves(offset, freq, self.row_whole)
        self.rows_psf = halves(self.lane_table(cosine, -sine, LANES, LANES))

        freq = np.arange(self.col_whole)
        place = np.concatenate([np.arange(cols + half), np.arange(-half, 0)])
        self.cols_out = halves(np.concatenate(waves(freq, place, self.col_whole)))
        self.cols_home = halves(np.concatenate(waves(np.arange(cols), freq, self.col_whole)))
        self.cols_psf = halves(np.concatenate(waves(freq, offset, self.col_whole)))

    @staticmethod
    def lane_table(real_part, imag_part, left, right):
        table = np.zeros((2 * left, 2 * right))
        height, width = real_part.shape
        table[:height, :width] = real_part
        table[:height, right : right + width] = imag_part
        table[left : left + height, :width] = -imag_part
        table[left : left + height, right : right + width] = real_part
        return table


def whole_spec(array):
    return pl.BlockSpec(array.shape, lambda i: (0,) * array.ndim)


def params():
    return pltpu.CompilerParams(
        dimension_semantics=("arbitrary",), vmem_limit_bytes=VMEM_LIMIT
    )


def cost(flops, moved):
    return pl.CostEstimate(flops=int(flops), bytes_accessed=int(moved), transcendentals=0)


def depth_out_kernel(plan, volume_ref, table_ref, out_ref):
    pad = jnp.zeros((LANES - plan.row_whole, plan.depth), jnp.float32)
    for j in range(ROWS):
        slab = volume_ref[:, j, :]
        if plan.row_whole < LANES:
            slab = jnp.concatenate([slab, pad], 0)
        result = table_by(table_ref, slab, ((1,), (1,)))
        out_ref[:, j, :LANES] = result[: plan.modes]
        out_ref[:, j, LANES:] = result[plan.mode_pad : plan.mode_pad + plan.modes]


def depth_out(plan, volume):
    return pl.pallas_call(
        functools.partial(depth_out_kernel, plan),
        grid=(plan.col_whole // ROWS,),
        in_specs=[
            pl.BlockSpec((plan.row_whole, ROWS, plan.depth), lambda i: (0, i, 0)),
            whole_spec(plan.depth_out),
        ],
        out_specs=pl.BlockSpec((plan.modes, ROWS, 2 * LANES), lambda i: (0, i, 0)),
        out_shape=jax.ShapeDtypeStruct((plan.modes, plan.col_whole, 2 * LANES), jnp.float32),
        compiler_params=params(),
        cost_estimate=cost(3e9, 2e7),
        name="depth_out",
    )(volume, plan.depth_out)


def turned(table, value, forward):
    both = table_by(table, value)
    half = both.shape[0] // 2
    cos_real, cos_imag = both[:half, :LANES], both[:half, LANES:]
    sin_real, sin_imag = both[half:, :LANES], both[half:, LANES:]
    if forward:
        return cos_real + sin_imag, cos_imag - sin_real
    return cos_real - sin_imag, cos_imag + sin_real


def transfer_kernel(psf_ref, rows_ref, cols_ref, out_ref):
    for j in range(out_ref.shape[0]):
        value = by_table(psf_ref[j], rows_ref)
        real_part, imag_part = turned(cols_ref, value, True)
        out_ref[j, :, :LANES] = real_part
        out_ref[j, :, LANES:] = imag_part


def step_of(modes):
    return max(size for size in range(1, 6) if modes % size == 0)


def transfer(plan, psf):
    edge = plan.edge
    offset = np.arange(edge) - plan.half
    cosine, sine = waves(offset, np.arange(plan.modes), plan.depth)
    parts = [
        jnp.einsum(
            "abc,ck->kba",
            psf,
            jnp.asarray(table, jnp.float32),
            precision=lax.Precision.HIGHEST,
        )
        for table in (cosine, -sine)
    ]
    parts = [jnp.pad(part, ((0, 0), (0, 0), (0, LANES - edge))) for part in parts]
    modes = jnp.concatenate(parts, 2)
    step = step_of(plan.modes)
    return pl.pallas_call(
        transfer_kernel,
        grid=(plan.modes // step,),
        in_specs=[
            pl.BlockSpec((step, edge, 2 * LANES), lambda i: (i, 0, 0)),
            whole_spec(plan.rows_psf),
            whole_spec(plan.cols_psf),
        ],
        out_specs=pl.BlockSpec((step, plan.col_whole, 2 * LANES), lambda i: (i, 0, 0)),
        out_shape=jax.ShapeDtypeStruct((plan.modes, plan.col_whole, 2 * LANES), jnp.float32),
        compiler_params=params(),
        cost_estimate=cost(9e9, 1.4e7),
        name="transfer",
    )(modes, plan.rows_psf, plan.cols_psf)


def filter_kernel(adjoint, modes_ref, transfer_ref, rows_out, cols_out, cols_home, rows_home, out_ref):
    for j in range(out_ref.shape[0]):
        value = by_table(modes_ref[j], rows_out)
        real_part, imag_part = turned(cols_out, value, True)
        gain_real = transfer_ref[j, :, :LANES]
        gain_imag = transfer_ref[j, :, LANES:]
        if adjoint:
            gain_imag = -gain_imag
        value = jnp.concatenate(
            [
                real_part * gain_real - imag_part * gain_imag,
                real_part * gain_imag + imag_part * gain_real,
            ],
            1,
        )
        value = jnp.concatenate(turned(cols_home, value, False), 1)
        out_ref[j] = by_table(value, rows_home)


def filtered(plan, modes, gains, adjoint):
    step = step_of(plan.modes)
    block = pl.BlockSpec((step, plan.col_whole, 2 * LANES), lambda i: (i, 0, 0))
    tables = [plan.rows_out, plan.cols_out, plan.cols_home, plan.rows_home]
    return pl.pallas_call(
        functools.partial(filter_kernel, adjoint),
        grid=(plan.modes // step,),
        in_specs=[block, block] + [whole_spec(table) for table in tables],
        out_specs=pl.BlockSpec((step, plan.cols, 2 * plan.rows), lambda i: (i, 0, 0)),
        out_shape=jax.ShapeDtypeStruct((plan.modes, plan.cols, 2 * plan.rows), jnp.float32),
        compiler_params=params(),
        cost_estimate=cost(2.2e10, 2.5e7),
        name="filtered",
    )(modes, gains, *tables)


def depth_home_kernel(plan, divide, modes_ref, other_ref, table_ref, out_ref):
    pad = jnp.zeros((plan.mode_pad - plan.modes, 2 * plan.rows), jnp.float32)
    for j in range(ROWS):
        slab = jnp.concatenate([modes_ref[:, j, :], pad], 0).T
        both = by_table(slab, table_ref)
        result = both[: plan.rows, : plan.depth] + both[plan.rows :, plan.depth :]
        other = other_ref[:, j, :]
        out_ref[:, j, :] = other / result if divide else other * result


def depth_home(plan, modes, other, divide):
    block = pl.BlockSpec((plan.rows, ROWS, plan.depth), lambda i: (0, i, 0))
    return pl.pallas_call(
        functools.partial(depth_home_kernel, plan, divide),
        grid=(plan.cols // ROWS,),
        in_specs=[
            pl.BlockSpec((plan.modes, ROWS, 2 * plan.rows), lambda i: (0, i, 0)),
            block,
            whole_spec(plan.depth_home),
        ],
        out_specs=block,
        out_shape=jax.ShapeDtypeStruct((plan.rows, plan.cols, plan.depth), jnp.float32),
        compiler_params=params(),
        cost_estimate=cost(3e9, 1.3e7),
        name="depth_home",
    )(modes, other, plan.depth_home)


def with_halo(block, width):
    row_count = lax.axis_size("px")
    col_count = lax.axis_size("py")
    devices = [(i, j) for i in range(row_count) for j in range(col_count)]

    def part(size, side):
        return {0: slice(None), 1: slice(0, width), -1: slice(size - width, size)}[side]

    def fetch(row_side, col_side):
        piece = block[part(block.shape[0], row_side), part(block.shape[1], col_side)]
        if row_side == 0 and col_side == 0:
            return piece
        pairs = [
            (
                ((i + row_side) % row_count) * col_count + (j + col_side) % col_count,
                i * col_count + j,
            )
            for i, j in devices
        ]
        return lax.ppermute(piece, ("px", "py"), pairs)

    sides = (0, 1, -1)
    return jnp.concatenate(
        [jnp.concatenate([fetch(row, col) for col in sides], 1) for row in sides], 0
    )


def variation(padded, row_count, col_count, row_whole, col_whole):
    region = padded[:-1, :-1]
    row_global = lax.axis_index("px") * row_count - 1 + jnp.arange(row_count + 1)
    col_global = lax.axis_index("py") * col_count - 1 + jnp.arange(col_count + 1)
    row_valid = ((row_global >= 0) & (row_global <= row_whole - 2))[:, None, None]
    col_valid = ((col_global >= 0) & (col_global <= col_whole - 2))[None, :, None]
    slope_rows = jnp.where(row_valid, padded[1:, :-1] - region, 0.0)
    slope_cols = jnp.where(col_valid, padded[:-1, 1:] - region, 0.0)
    slope_depth = jnp.concatenate(
        [region[:, :, 1:] - region[:, :, :-1], jnp.zeros_like(region[:, :, :1])], 2
    )
    factor = lax.rsqrt(
        slope_rows * slope_rows
        + slope_cols * slope_cols
        + slope_depth * slope_depth
        + smoothing * smoothing
    )
    flux_rows = slope_rows * factor
    flux_cols = slope_cols * factor
    flux_depth = (slope_depth * factor)[1:, 1:]
    before = jnp.concatenate([jnp.zeros_like(flux_depth[:, :, :1]), flux_depth[:, :, :-1]], 2)
    return (
        flux_rows[1:, 1:]
        - flux_rows[:-1, 1:]
        + (flux_cols[1:, 1:] - flux_cols[1:, :-1])
        + (flux_depth - before)
    )


def ring(padded, rows, cols):
    padded = jnp.concatenate([padded[-1:], padded[: rows + 1]], 0)
    return jnp.concatenate([padded[:, -1:], padded[:, : cols + 1]], 1)


def shards(estimate, observed, psf):
    rows, cols, depth = estimate.shape
    plan = Plan(rows, cols, depth, psf.shape[0])
    gains = transfer(plan, psf)
    padded = with_halo(estimate, plan.half)
    modes = filtered(plan, depth_out(plan, padded), gains, False)
    quotient = depth_home(plan, modes, observed, True)
    divergence = variation(
        ring(padded, rows, cols),
        rows,
        cols,
        rows * lax.axis_size("px"),
        cols * lax.axis_size("py"),
    )
    weight = estimate / (1.0 - penalty_weight * divergence)
    modes = filtered(plan, depth_out(plan, with_halo(quotient, plan.half)), gains, True)
    return depth_home(plan, modes, weight, False)


def solution(mesh):
    placed = (P("px", "py", None), P("px", "py", None), P())
    return jax.shard_map(
        shards, mesh=mesh, in_specs=placed, out_specs=P("px", "py", None), check_vma=False
    )
```

```python
import functools
import math

import jax
import jax.numpy as jnp
import ml_dtypes
import numpy as np
from jax import lax
from jax.experimental import pallas as pl
from jax.experimental.pallas import tpu as pltpu
from jax.sharding import PartitionSpec as P

penalty_weight = 0.1
smoothing = 0.1

LANES = 128
ROWS = 8
VMEM_LIMIT = 48 * 1024 * 1024


def halves(table):
    table = np.asarray(table, np.float64).astype(np.float32)
    high = table.astype(ml_dtypes.bfloat16)
    low = (table - high.astype(np.float32)).astype(ml_dtypes.bfloat16)
    return high, low


def thrice(table, axis):
    high, low = halves(table)
    return np.concatenate([high, high, low], axis)


def waves(left, right, length):
    turns = np.remainder(np.outer(left, right), length) * (2.0 * math.pi / length)
    return np.cos(turns), np.sin(turns)


def up16(count):
    return -(-count // 16) * 16


def split(value):
    high = value.astype(jnp.bfloat16)
    low = (value - high.astype(jnp.float32)).astype(jnp.bfloat16)
    return high, low


def dot(left, right, dims=((1,), (0,))):
    return lax.dot_general(left, right, (dims, ((), ())), preferred_element_type=jnp.float32)


def by_table(value, table):
    high, low = split(value)
    return dot(jnp.concatenate([high, low, high], 1), table)


def table_by(table, value):
    high, low = split(value)
    return dot(table, jnp.concatenate([high, low, high], 0))


class Plan:
    def __init__(self, rows, cols, depth, edge):
        half = edge // 2
        self.rows, self.cols, self.depth, self.edge, self.half = rows, cols, depth, edge, half
        self.row_whole = rows + edge
        self.col_whole = cols + edge
        self.modes = depth // 2 + 1
        self.mode_pad = up16(self.modes)
        self.mode_step = -(-self.modes // ROWS) * ROWS
        modes = np.arange(self.modes)

        cosine, sine = waves(modes, np.arange(depth), depth)
        table = np.zeros((up16(2 * self.mode_step), depth))
        table[: self.modes] = cosine
        table[self.mode_step : self.mode_step + self.modes] = -sine
        self.depth_out = thrice(table, 1)
        weight = np.where((modes == 0) | (2 * modes == depth), 1.0, 2.0)
        weight = weight / (depth * self.row_whole * self.col_whole)
        table = np.zeros((self.mode_pad, 2 * depth))
        table[: self.modes, :depth] = cosine * weight[:, None]
        table[: self.modes, depth:] = -sine * weight[:, None]
        self.depth_home = thrice(table, 0)

        freq = np.arange(self.row_whole)
        place = np.concatenate([np.arange(rows + half), np.arange(-half, 0)])
        cosine, sine = waves(place, freq, self.row_whole)
        self.rows_out = thrice(self.lane_table(cosine, -sine, LANES, LANES), 0)
        cosine, sine = waves(freq, np.arange(rows), self.row_whole)
        self.rows_home = thrice(self.lane_table(cosine, sine, LANES, rows), 0)
        offset = np.arange(edge) - half
        cosine, sine = waves(offset, freq, self.row_whole)
        self.rows_psf = thrice(self.lane_table(cosine, -sine, LANES, LANES), 0)

        freq = np.arange(self.col_whole)
        place = np.concatenate([np.arange(cols + half), np.arange(-half, 0)])
        self.cols_out = thrice(np.concatenate(waves(freq, place, self.col_whole)), 1)
        self.cols_home = thrice(np.concatenate(waves(np.arange(cols), freq, self.col_whole)), 1)
        self.cols_psf = thrice(np.concatenate(waves(freq, offset, self.col_whole)), 1)

    @staticmethod
    def lane_table(real_part, imag_part, left, right):
        table = np.zeros((2 * left, 2 * right))
        height, width = real_part.shape
        table[:height, :width] = real_part
        table[:height, right : right + width] = imag_part
        table[left : left + height, :width] = -imag_part
        table[left : left + height, right : right + width] = real_part
        return table


def whole_spec(array):
    return pl.BlockSpec(array.shape, lambda i: (0,) * array.ndim)


def params():
    return pltpu.CompilerParams(
        dimension_semantics=("arbitrary",), vmem_limit_bytes=VMEM_LIMIT
    )


def cost(flops, moved):
    return pl.CostEstimate(flops=int(flops), bytes_accessed=int(moved), transcendentals=0)


def depth_out_kernel(plan, volume_ref, table_ref, out_ref):
    volume = volume_ref.reshape(plan.row_whole * ROWS, plan.depth)
    out = out_ref.reshape(plan.modes * 2 * ROWS, LANES)
    pad = jnp.zeros((LANES - plan.row_whole, plan.depth), jnp.float32)
    depth = plan.depth
    for j in range(0, ROWS, 2):
        slabs = []
        for row in (j, j + 1):
            slabs.append(volume[pl.ds(row, plan.row_whole, stride=ROWS), :])
            if plan.row_whole < LANES:
                slabs.append(pad)
        high, low = split(jnp.concatenate(slabs, 0))
        across = ((1,), (1,))
        result = dot(table_ref[:, : 2 * depth], jnp.concatenate([high, low], 1), across)
        result = result + dot(table_ref[:, 2 * depth :], high, across)
        for c in range(2):
            part = result[c * plan.mode_step : c * plan.mode_step + plan.modes]
            for row in range(2):
                out[pl.ds(c * ROWS + j + row, plan.modes, stride=2 * ROWS), :] = part[
                    :, row * LANES : (row + 1) * LANES
                ]


def depth_out(plan, volume):
    return pl.pallas_call(
        functools.partial(depth_out_kernel, plan),
        grid=(plan.col_whole // ROWS,),
        in_specs=[
            pl.BlockSpec((plan.row_whole, ROWS, plan.depth), lambda i: (0, i, 0)),
            whole_spec(plan.depth_out),
        ],
        out_specs=pl.BlockSpec((plan.modes, 2, ROWS, LANES), lambda i: (0, 0, i, 0)),
        out_shape=jax.ShapeDtypeStruct((plan.modes, 2, plan.col_whole, LANES), jnp.float32),
        compiler_params=params(),
        cost_estimate=cost(3e9, 2e7),
        name="depth_out",
    )(volume, plan.depth_out)


def turned(table, value, forward):
    both = table_by(table, value)
    half = both.shape[0] // 2
    cos_real, cos_imag = both[:half, :LANES], both[:half, LANES:]
    sin_real, sin_imag = both[half:, :LANES], both[half:, LANES:]
    if forward:
        return cos_real + sin_imag, cos_imag - sin_real
    return cos_real - sin_imag, cos_imag + sin_real


def transfer_kernel(psf_ref, rows_ref, cols_ref, out_ref):
    step, edge = psf_ref.shape[:2]
    values = by_table(jnp.concatenate([psf_ref[j] for j in range(step)], 0), rows_ref[...])
    for j in range(step):
        value = values[j * edge : (j + 1) * edge]
        out_ref[j] = jnp.concatenate(turned(cols_ref[...], value, True), 1)


def step_of(modes):
    return max(size for size in range(1, 6) if modes % size == 0)


def transfer(plan, psf):
    edge = plan.edge
    offset = np.arange(edge) - plan.half
    cosine, sine = waves(offset, np.arange(plan.modes), plan.depth)
    parts = [
        jnp.einsum(
            "abc,ck->kba",
            psf,
            jnp.asarray(table, jnp.float32),
            precision=lax.Precision.HIGHEST,
        )
        for table in (cosine, -sine)
    ]
    parts = [jnp.pad(part, ((0, 0), (0, 0), (0, LANES - edge))) for part in parts]
    modes = jnp.concatenate(parts, 2)
    step = step_of(plan.modes)
    return pl.pallas_call(
        transfer_kernel,
        grid=(plan.modes // step,),
        in_specs=[
            pl.BlockSpec((step, edge, 2 * LANES), lambda i: (i, 0, 0)),
            whole_spec(plan.rows_psf),
            whole_spec(plan.cols_psf),
        ],
        out_specs=pl.BlockSpec((step, plan.col_whole, 2 * LANES), lambda i: (i, 0, 0)),
        out_shape=jax.ShapeDtypeStruct((plan.modes, plan.col_whole, 2 * LANES), jnp.float32),
        compiler_params=params(),
        cost_estimate=cost(9e9, 1.4e7),
        name="transfer",
    )(modes, plan.rows_psf, plan.cols_psf)


def filter_kernel(adjoint, modes_ref, transfer_ref, rows_out, cols_out, cols_home, rows_home, out_ref):
    step, _, size, _ = modes_ref.shape
    cols = out_ref.shape[1]
    slabs = [jnp.concatenate([modes_ref[j, 0], modes_ref[j, 1]], 1) for j in range(step)]
    values = by_table(jnp.concatenate(slabs, 0), rows_out[...])
    home = []
    for j in range(step):
        real_part, imag_part = turned(cols_out[...], values[j * size : (j + 1) * size], True)
        gain_real = transfer_ref[j, :, :LANES]
        gain_imag = transfer_ref[j, :, LANES:]
        if adjoint:
            gain_imag = -gain_imag
        value = jnp.concatenate(
            [
                real_part * gain_real - imag_part * gain_imag,
                real_part * gain_imag + imag_part * gain_real,
            ],
            1,
        )
        home.append(jnp.concatenate(turned(cols_home[...], value, False), 1))
    values = by_table(jnp.concatenate(home, 0), rows_home[...])
    for j in range(step):
        out_ref[j] = values[j * cols : (j + 1) * cols]


def filtered(plan, modes, gains, adjoint):
    step = step_of(plan.modes)
    block = pl.BlockSpec((step, plan.col_whole, 2 * LANES), lambda i: (i, 0, 0))
    modes_block = pl.BlockSpec((step, 2, plan.col_whole, LANES), lambda i: (i, 0, 0, 0))
    tables = [plan.rows_out, plan.cols_out, plan.cols_home, plan.rows_home]
    return pl.pallas_call(
        functools.partial(filter_kernel, adjoint),
        grid=(plan.modes // step,),
        in_specs=[modes_block, block] + [whole_spec(table) for table in tables],
        out_specs=pl.BlockSpec((step, plan.cols, 2 * plan.rows), lambda i: (i, 0, 0)),
        out_shape=jax.ShapeDtypeStruct((plan.modes, plan.cols, 2 * plan.rows), jnp.float32),
        compiler_params=params(),
        cost_estimate=cost(2.2e10, 2.5e7),
        name="filtered",
    )(modes, gains, *tables)


def depth_home_kernel(plan, divide, modes_ref, other_ref, table_ref, out_ref):
    lanes = 2 * plan.rows
    modes = modes_ref.reshape(plan.modes * ROWS, lanes)
    others = other_ref.reshape(plan.rows * ROWS, plan.depth)
    out = out_ref.reshape(plan.rows * ROWS, plan.depth)
    pad = jnp.zeros((plan.mode_pad - plan.modes, lanes), jnp.float32)
    for j in range(ROWS):
        slab = modes[pl.ds(j, plan.modes, stride=ROWS), :]
        high, low = split(jnp.concatenate([slab, pad], 0))
        slab = jnp.concatenate([high, low, high], 0)
        both = dot(slab, table_ref[...], ((0,), (0,)))
        result = both[: plan.rows, : plan.depth] + both[plan.rows :, plan.depth :]
        other = others[pl.ds(j, plan.rows, stride=ROWS), :]
        out[pl.ds(j, plan.rows, stride=ROWS), :] = other / result if divide else other * result


def depth_home(plan, modes, other, divide):
    block = pl.BlockSpec((plan.rows, ROWS, plan.depth), lambda i: (0, i, 0))
    return pl.pallas_call(
        functools.partial(depth_home_kernel, plan, divide),
        grid=(plan.cols // ROWS,),
        in_specs=[
            pl.BlockSpec((plan.modes, ROWS, 2 * plan.rows), lambda i: (0, i, 0)),
            block,
            whole_spec(plan.depth_home),
        ],
        out_specs=block,
        out_shape=jax.ShapeDtypeStruct((plan.rows, plan.cols, plan.depth), jnp.float32),
        compiler_params=params(),
        cost_estimate=cost(3e9, 1.3e7),
        name="depth_home",
    )(modes, other, plan.depth_home)


def with_halo(block, width):
    row_count = lax.axis_size("px")
    col_count = lax.axis_size("py")
    devices = [(i, j) for i in range(row_count) for j in range(col_count)]

    def part(size, side):
        return {0: slice(None), 1: slice(0, width), -1: slice(size - width, size)}[side]

    def fetch(row_side, col_side):
        piece = block[part(block.shape[0], row_side), part(block.shape[1], col_side)]
        if row_side == 0 and col_side == 0:
            return piece
        pairs = [
            (
                ((i + row_side) % row_count) * col_count + (j + col_side) % col_count,
                i * col_count + j,
            )
            for i, j in devices
        ]
        return lax.ppermute(piece, ("px", "py"), pairs)

    sides = (0, 1, -1)
    return jnp.concatenate(
        [jnp.concatenate([fetch(row, col) for col in sides], 1) for row in sides], 0
    )


def variation(padded, row_count, col_count, row_whole, col_whole):
    region = padded[:-1, :-1]
    row_global = lax.axis_index("px") * row_count - 1 + jnp.arange(row_count + 1)
    col_global = lax.axis_index("py") * col_count - 1 + jnp.arange(col_count + 1)
    row_valid = ((row_global >= 0) & (row_global <= row_whole - 2))[:, None, None]
    col_valid = ((col_global >= 0) & (col_global <= col_whole - 2))[None, :, None]
    slope_rows = jnp.where(row_valid, padded[1:, :-1] - region, 0.0)
    slope_cols = jnp.where(col_valid, padded[:-1, 1:] - region, 0.0)
    slope_depth = jnp.concatenate(
        [region[:, :, 1:] - region[:, :, :-1], jnp.zeros_like(region[:, :, :1])], 2
    )
    factor = lax.rsqrt(
        slope_rows * slope_rows
        + slope_cols * slope_cols
        + slope_depth * slope_depth
        + smoothing * smoothing
    )
    flux_rows = slope_rows * factor
    flux_cols = slope_cols * factor
    flux_depth = (slope_depth * factor)[1:, 1:]
    before = jnp.concatenate([jnp.zeros_like(flux_depth[:, :, :1]), flux_depth[:, :, :-1]], 2)
    return (
        flux_rows[1:, 1:]
        - flux_rows[:-1, 1:]
        + (flux_cols[1:, 1:] - flux_cols[1:, :-1])
        + (flux_depth - before)
    )


def ring(padded, rows, cols):
    padded = jnp.concatenate([padded[-1:], padded[: rows + 1]], 0)
    return jnp.concatenate([padded[:, -1:], padded[:, : cols + 1]], 1)


def shards(estimate, observed, psf):
    rows, cols, depth = estimate.shape
    plan = Plan(rows, cols, depth, psf.shape[0])
    gains = transfer(plan, psf)
    padded = with_halo(estimate, plan.half)
    modes = filtered(plan, depth_out(plan, padded), gains, False)
    quotient = depth_home(plan, modes, observed, True)
    divergence = variation(
        ring(padded, rows, cols),
        rows,
        cols,
        rows * lax.axis_size("px"),
        cols * lax.axis_size("py"),
    )
    weight = estimate / (1.0 - penalty_weight * divergence)
    modes = filtered(plan, depth_out(plan, with_halo(quotient, plan.half)), gains, True)
    return depth_home(plan, modes, weight, False)


def solution(mesh):
    placed = (P("px", "py", None), P("px", "py", None), P())
    return jax.shard_map(
        shards, mesh=mesh, in_specs=placed, out_specs=P("px", "py", None), check_vma=False
    )
```

```python
import functools
import math

import jax
import jax.numpy as jnp
import ml_dtypes
import numpy as np
from jax import lax
from jax.experimental import pallas as pl
from jax.experimental.pallas import tpu as pltpu
from jax.sharding import PartitionSpec as P

penalty_weight = 0.1
smoothing = 0.1

LANES = 128
HALF = LANES // 2
ROWS = 8
VMEM_LIMIT = 48 * 1024 * 1024


def halves(table):
    table = np.asarray(table, np.float64).astype(np.float32)
    high = table.astype(ml_dtypes.bfloat16)
    low = (table - high.astype(np.float32)).astype(ml_dtypes.bfloat16)
    return high, low


def thrice(table, axis):
    high, low = halves(table)
    return np.concatenate([high, high, low], axis)


def waves(left, right, length):
    turns = np.remainder(np.outer(left, right), length) * (2.0 * math.pi / length)
    return np.cos(turns), np.sin(turns)


def up16(count):
    return -(-count // 16) * 16


def split(value):
    high = value.astype(jnp.bfloat16)
    low = (value - high.astype(jnp.float32)).astype(jnp.bfloat16)
    return high, low


def dot(left, right, dims=((1,), (0,))):
    return lax.dot_general(left, right, (dims, ((), ())), preferred_element_type=jnp.float32)


def by_table(value, table):
    high, low = split(value)
    return dot(jnp.concatenate([high, low, high], 1), table)


def table_by(table, value):
    high, low = split(value)
    return dot(table, jnp.concatenate([high, low, high], 0))


class Plan:
    def __init__(self, rows, cols, depth, edge):
        half = edge // 2
        self.rows, self.cols, self.depth, self.edge, self.half = rows, cols, depth, edge, half
        self.row_whole = rows + edge
        self.col_whole = cols + edge
        self.modes = depth // 2 + 1
        self.mode_pad = up16(self.modes)
        self.mode_step = -(-self.modes // ROWS) * ROWS
        modes = np.arange(self.modes)

        cosine, sine = waves(modes, np.arange(depth), depth)
        table = np.zeros((up16(2 * self.mode_step), depth))
        table[: self.modes] = cosine
        table[self.mode_step : self.mode_step + self.modes] = -sine
        self.depth_out = thrice(table, 1)
        weight = np.where((modes == 0) | (2 * modes == depth), 1.0, 2.0)
        weight = weight / (depth * self.row_whole * self.col_whole)
        table = np.zeros((self.mode_pad, 2 * depth))
        table[: self.modes, :depth] = cosine * weight[:, None]
        table[: self.modes, depth:] = -sine * weight[:, None]
        self.depth_home = thrice(table, 0)

        freq = np.arange(self.row_whole)
        own = self.lane_table(*self.out_waves(np.arange(rows), freq), HALF, LANES)
        place = np.concatenate([np.arange(rows, rows + half), np.arange(-half, 0)])
        halo = self.lane_table(*self.out_waves(place, freq), HALF, LANES)
        self.rows_out = thrice(np.concatenate([own, halo]), 0)
        cosine, sine = waves(freq, np.arange(rows), self.row_whole)
        self.rows_home = thrice(self.lane_table(cosine, sine, LANES, rows), 0)
        offset = np.arange(edge) - half
        self.rows_psf = thrice(self.lane_table(*self.out_waves(offset, freq), LANES, LANES), 0)

        freq = np.arange(self.col_whole)
        place = np.concatenate([np.arange(cols + half), np.arange(-half, 0)])
        self.cols_out = thrice(np.concatenate(waves(freq, place, self.col_whole)), 1)
        self.cols_home = thrice(np.concatenate(waves(np.arange(cols), freq, self.col_whole)), 1)
        self.cols_psf = thrice(np.concatenate(waves(freq, offset, self.col_whole)), 1)

    def out_waves(self, place, freq):
        cosine, sine = waves(place, freq, self.row_whole)
        return cosine, -sine

    @staticmethod
    def lane_table(real_part, imag_part, left, right):
        table = np.zeros((2 * left, 2 * right))
        height, width = real_part.shape
        table[:height, :width] = real_part
        table[:height, right : right + width] = imag_part
        table[left : left + height, :width] = -imag_part
        table[left : left + height, right : right + width] = real_part
        return table


def whole_spec(array):
    return pl.BlockSpec(array.shape, lambda i: (0,) * array.ndim)


def params():
    return pltpu.CompilerParams(
        dimension_semantics=("arbitrary",), vmem_limit_bytes=VMEM_LIMIT
    )


def cost(flops, moved):
    return pl.CostEstimate(flops=int(flops), bytes_accessed=int(moved), transcendentals=0)


def depth_out_kernel(plan, count, *refs):
    pieces, table_ref, out_ref = refs[:count], refs[count], refs[count + 1]
    sizes = [piece.shape[0] for piece in pieces]
    pieces = [piece.reshape(piece.shape[0] * ROWS, plan.depth) for piece in pieces]
    out = out_ref.reshape(plan.modes * ROWS, LANES)
    size = sum(sizes)
    group = min(ROWS, 2 * LANES // size)
    depth = plan.depth
    across = ((1,), (1,))
    for first in range(0, ROWS, group):
        slabs = [
            piece[pl.ds(j, length, stride=ROWS), :]
            for j in range(first, first + group)
            for piece, length in zip(pieces, sizes)
        ]
        high, low = split(jnp.concatenate(slabs, 0))
        result = dot(table_ref[:, : 2 * depth], jnp.concatenate([high, low], 1), across)
        result = result + dot(table_ref[:, 2 * depth :], high, across)
        real_part = result[: plan.modes]
        imag_part = result[plan.mode_step : plan.mode_step + plan.modes]
        gap = [jnp.zeros((plan.modes, HALF - size), jnp.float32)] if size < HALF else []
        for j in range(group):
            lanes = slice(j * size, (j + 1) * size)
            value = jnp.concatenate([real_part[:, lanes], *gap, imag_part[:, lanes], *gap], 1)
            out[pl.ds(first + j, plan.modes, stride=ROWS), :] = value


def depth_out(plan, name, *pieces):
    cols = pieces[0].shape[1]
    return pl.pallas_call(
        functools.partial(depth_out_kernel, plan, len(pieces)),
        grid=(cols // ROWS,),
        in_specs=[
            pl.BlockSpec((piece.shape[0], ROWS, plan.depth), lambda i: (0, i, 0))
            for piece in pieces
        ]
        + [whole_spec(plan.depth_out)],
        out_specs=pl.BlockSpec((plan.modes, ROWS, LANES), lambda i: (0, i, 0)),
        out_shape=jax.ShapeDtypeStruct((plan.modes, cols, LANES), jnp.float32),
        compiler_params=params(),
        cost_estimate=cost(6e7 * cols, 7e4 * cols),
        name=name,
    )(*pieces, plan.depth_out)


def turned_narrow(table, planes):
    both = table_by(table, jnp.concatenate(planes, 1) if len(planes) > 1 else planes[0])
    half = both.shape[0] // 2
    lane = lax.broadcasted_iota(jnp.int32, (half, LANES), 1)
    out = []
    for j in range(len(planes)):
        cosine = both[:half, j * LANES : (j + 1) * LANES]
        sine = pltpu.roll(both[half:, j * LANES : (j + 1) * LANES], HALF, 1)
        out.append(cosine + jnp.where(lane < HALF, sine, -sine))
    return out


def pairs_of(count):
    return [range(j, min(j + 2, count)) for j in range(0, count, 2)]


def cols_kernel(inner_ref, outer_ref, table_ref, out_ref):
    for pair in pairs_of(out_ref.shape[0]):
        planes = [jnp.concatenate([inner_ref[j], outer_ref[j]], 0) for j in pair]
        for j, plane in zip(pair, turned_narrow(table_ref[...], planes)):
            out_ref[j] = plane


def cols_out(plan, inner, outer):
    step = step_of(plan.modes, 13)

    def spec(size):
        return pl.BlockSpec((step, size, LANES), lambda i: (i, 0, 0))

    return pl.pallas_call(
        cols_kernel,
        grid=(plan.modes // step,),
        in_specs=[spec(plan.cols), spec(plan.edge), whole_spec(plan.cols_out)],
        out_specs=spec(plan.col_whole),
        out_shape=jax.ShapeDtypeStruct((plan.modes, plan.col_whole, LANES), jnp.float32),
        compiler_params=params(),
        cost_estimate=cost(8e9, 1.1e7),
        name="cols_out",
    )(inner, outer, plan.cols_out)


def turned(table, value, forward):
    both = table_by(table, value)
    half = both.shape[0] // 2
    cos_real, cos_imag = both[:half, :LANES], both[:half, LANES:]
    sin_real, sin_imag = both[half:, :LANES], both[half:, LANES:]
    if forward:
        return cos_real + sin_imag, cos_imag - sin_real
    return cos_real - sin_imag, cos_imag + sin_real


def transfer_kernel(psf_ref, rows_ref, cols_ref, out_ref):
    step, edge = psf_ref.shape[:2]
    values = by_table(jnp.concatenate([psf_ref[j] for j in range(step)], 0), rows_ref[...])
    for j in range(step):
        value = values[j * edge : (j + 1) * edge]
        out_ref[j] = jnp.concatenate(turned(cols_ref[...], value, True), 1)


def step_of(modes, most):
    return max(size for size in range(1, most + 1) if modes % size == 0)


def transfer(plan, psf):
    edge = plan.edge
    offset = np.arange(edge) - plan.half
    cosine, sine = waves(offset, np.arange(plan.modes), plan.depth)
    parts = [
        jnp.einsum(
            "abc,ck->kba",
            psf,
            jnp.asarray(table, jnp.float32),
            precision=lax.Precision.HIGHEST,
        )
        for table in (cosine, -sine)
    ]
    parts = [jnp.pad(part, ((0, 0), (0, 0), (0, LANES - edge))) for part in parts]
    modes = jnp.concatenate(parts, 2)
    step = step_of(plan.modes, 5)
    return pl.pallas_call(
        transfer_kernel,
        grid=(plan.modes // step,),
        in_specs=[
            pl.BlockSpec((step, edge, 2 * LANES), lambda i: (i, 0, 0)),
            whole_spec(plan.rows_psf),
            whole_spec(plan.cols_psf),
        ],
        out_specs=pl.BlockSpec((step, plan.col_whole, 2 * LANES), lambda i: (i, 0, 0)),
        out_shape=jax.ShapeDtypeStruct((plan.modes, plan.col_whole, 2 * LANES), jnp.float32),
        compiler_params=params(),
        cost_estimate=cost(9e9, 1.4e7),
        name="transfer",
    )(modes, plan.rows_psf, plan.cols_psf)


def filter_kernel(
    adjoint, own_ref, inner_ref, outer_ref, transfer_ref,
    rows_out, cols_out, cols_home, rows_home, out_ref,
):
    step, size, _ = own_ref.shape
    cols = out_ref.shape[1]
    slabs = []
    for pair in pairs_of(step):
        planes = [jnp.concatenate([inner_ref[j], outer_ref[j]], 0) for j in pair]
        for j, plane in zip(pair, turned_narrow(cols_out[...], planes)):
            slabs.append(jnp.concatenate([own_ref[j], plane], 1))
    values = by_table(jnp.concatenate(slabs, 0), rows_out[...])
    home = []
    for j in range(step):
        real_part = values[j * size : (j + 1) * size, :LANES]
        imag_part = values[j * size : (j + 1) * size, LANES:]
        gain_real = transfer_ref[j, :, :LANES]
        gain_imag = transfer_ref[j, :, LANES:]
        if adjoint:
            gain_imag = -gain_imag
        value = jnp.concatenate(
            [
                real_part * gain_real - imag_part * gain_imag,
                real_part * gain_imag + imag_part * gain_real,
            ],
            1,
        )
        home.append(jnp.concatenate(turned(cols_home[...], value, False), 1))
    values = by_table(jnp.concatenate(home, 0), rows_home[...])
    for j in range(step):
        out_ref[j] = values[j * cols : (j + 1) * cols]


def filtered(plan, own, inner, outer, gains, adjoint):
    step = step_of(plan.modes, 5)
    block = pl.BlockSpec((step, plan.col_whole, 2 * LANES), lambda i: (i, 0, 0))

    def spec(size):
        return pl.BlockSpec((step, size, LANES), lambda i: (i, 0, 0))

    tables = [plan.rows_out, plan.cols_out, plan.cols_home, plan.rows_home]
    return pl.pallas_call(
        functools.partial(filter_kernel, adjoint),
        grid=(plan.modes // step,),
        in_specs=[spec(plan.col_whole), spec(plan.cols), spec(plan.edge), block]
        + [whole_spec(table) for table in tables],
        out_specs=pl.BlockSpec((step, plan.cols, 2 * plan.rows), lambda i: (i, 0, 0)),
        out_shape=jax.ShapeDtypeStruct((plan.modes, plan.cols, 2 * plan.rows), jnp.float32),
        compiler_params=params(),
        cost_estimate=cost(2.2e10, 2.5e7),
        name="filtered",
    )(own, inner, outer, gains, *tables)


def depth_home_kernel(plan, divide, modes_ref, other_ref, table_ref, out_ref):
    lanes = 2 * plan.rows
    modes = modes_ref.reshape(plan.modes * ROWS, lanes)
    others = other_ref.reshape(plan.rows * ROWS, plan.depth)
    out = out_ref.reshape(plan.rows * ROWS, plan.depth)
    pad = jnp.zeros((plan.mode_pad - plan.modes, lanes), jnp.float32)
    for j in range(ROWS):
        slab = modes[pl.ds(j, plan.modes, stride=ROWS), :]
        high, low = split(jnp.concatenate([slab, pad], 0))
        slab = jnp.concatenate([high, low, high], 0)
        both = dot(slab, table_ref[...], ((0,), (0,)))
        result = both[: plan.rows, : plan.depth] + both[plan.rows :, plan.depth :]
        other = others[pl.ds(j, plan.rows, stride=ROWS), :]
        out[pl.ds(j, plan.rows, stride=ROWS), :] = other / result if divide else other * result


def depth_home(plan, modes, other, divide):
    block = pl.BlockSpec((plan.rows, ROWS, plan.depth), lambda i: (0, i, 0))
    return pl.pallas_call(
        functools.partial(depth_home_kernel, plan, divide),
        grid=(plan.cols // ROWS,),
        in_specs=[
            pl.BlockSpec((plan.modes, ROWS, 2 * plan.rows), lambda i: (0, i, 0)),
            block,
            whole_spec(plan.depth_home),
        ],
        out_specs=block,
        out_shape=jax.ShapeDtypeStruct((plan.rows, plan.cols, plan.depth), jnp.float32),
        compiler_params=params(),
        cost_estimate=cost(3e9, 1.3e7),
        name="depth_home",
    )(modes, other, plan.depth_home)


def neighbours(axis, after, before):
    count = lax.axis_size(axis)
    return (
        lax.ppermute(after, axis, [((i + 1) % count, i) for i in range(count)]),
        lax.ppermute(before, axis, [(i, (i + 1) % count) for i in range(count)]),
    )


def halos(block, width):
    rows = neighbours("px", block[:width], block[-width:])
    cols = jnp.concatenate(neighbours("py", block[:, :width], block[:, -width:]), 1)
    corners = neighbours("px", cols[:width], cols[-width:])
    return rows, cols, corners


def convolved(plan, block, around, gains, adjoint):
    rows, cols, corners = around
    own = cols_out(
        plan, depth_out(plan, "depth_own", block), depth_out(plan, "depth_cols", cols)
    )
    inner = depth_out(plan, "depth_rows", *rows)
    outer = depth_out(plan, "depth_corners", *corners)
    return filtered(plan, own, inner, outer, gains, adjoint)


def variation(padded, row_count, col_count, row_whole, col_whole):
    region = padded[:-1, :-1]
    row_global = lax.axis_index("px") * row_count - 1 + jnp.arange(row_count + 1)
    col_global = lax.axis_index("py") * col_count - 1 + jnp.arange(col_count + 1)
    row_valid = ((row_global >= 0) & (row_global <= row_whole - 2))[:, None, None]
    col_valid = ((col_global >= 0) & (col_global <= col_whole - 2))[None, :, None]
    slope_rows = jnp.where(row_valid, padded[1:, :-1] - region, 0.0)
    slope_cols = jnp.where(col_valid, padded[:-1, 1:] - region, 0.0)
    slope_depth = jnp.concatenate(
        [region[:, :, 1:] - region[:, :, :-1], jnp.zeros_like(region[:, :, :1])], 2
    )
    factor = lax.rsqrt(
        slope_rows * slope_rows
        + slope_cols * slope_cols
        + slope_depth * slope_depth
        + smoothing * smoothing
    )
    flux_rows = slope_rows * factor
    flux_cols = slope_cols * factor
    flux_depth = (slope_depth * factor)[1:, 1:]
    before = jnp.concatenate([jnp.zeros_like(flux_depth[:, :, :1]), flux_depth[:, :, :-1]], 2)
    return (
        flux_rows[1:, 1:]
        - flux_rows[:-1, 1:]
        + (flux_cols[1:, 1:] - flux_cols[1:, :-1])
        + (flux_depth - before)
    )


def ring(block, around):
    rows, cols, corners = around
    after = jnp.concatenate([corners[0][:1, -1:], rows[0][:1], corners[0][:1, :1]], 1)
    before = jnp.concatenate([corners[1][-1:, -1:], rows[1][-1:], corners[1][-1:, :1]], 1)
    middle = jnp.concatenate([cols[:, -1:], block, cols[:, :1]], 1)
    return jnp.concatenate([before, middle, after], 0)


def shards(estimate, observed, psf):
    rows, cols, depth = estimate.shape
    plan = Plan(rows, cols, depth, psf.shape[0])
    around = halos(estimate, plan.half)
    gains = transfer(plan, psf)
    modes = convolved(plan, estimate, around, gains, False)
    quotient = depth_home(plan, modes, observed, True)
    quotient_around = halos(quotient, plan.half)
    divergence = variation(
        ring(estimate, around),
        rows,
        cols,
        rows * lax.axis_size("px"),
        cols * lax.axis_size("py"),
    )
    weight = estimate / (1.0 - penalty_weight * divergence)
    modes = convolved(plan, quotient, quotient_around, gains, True)
    return depth_home(plan, modes, weight, False)


def solution(mesh):
    placed = (P("px", "py", None), P("px", "py", None), P())
    return jax.shard_map(
        shards, mesh=mesh, in_specs=placed, out_specs=P("px", "py", None), check_vma=False
    )
```

```python
import functools
import math

import jax
import jax.numpy as jnp
import ml_dtypes
import numpy as np
from jax import lax
from jax.experimental import pallas as pl
from jax.experimental.pallas import tpu as pltpu
from jax.sharding import PartitionSpec as P

penalty_weight = 0.1
smoothing = 0.1

LANES = 128
HALF = LANES // 2
ROWS = 8
VMEM_LIMIT = 48 * 1024 * 1024


def halves(table):
    table = np.asarray(table, np.float64).astype(np.float32)
    high = table.astype(ml_dtypes.bfloat16)
    low = (table - high.astype(np.float32)).astype(ml_dtypes.bfloat16)
    return high, low


def thrice(table, axis):
    high, low = halves(table)
    return np.concatenate([high, high, low], axis)


def waves(left, right, length):
    turns = np.remainder(np.outer(left, right), length) * (2.0 * math.pi / length)
    return np.cos(turns), np.sin(turns)


def up16(count):
    return -(-count // 16) * 16


def split(value):
    high = value.astype(jnp.bfloat16)
    low = (value - high.astype(jnp.float32)).astype(jnp.bfloat16)
    return high, low


def dot(left, right, dims=((1,), (0,))):
    return lax.dot_general(left, right, (dims, ((), ())), preferred_element_type=jnp.float32)


def by_table(value, table):
    high, low = split(value)
    return dot(jnp.concatenate([high, low, high], 1), table)


def table_by(table, value):
    high, low = split(value)
    return dot(table, jnp.concatenate([high, low, high], 0))


class Plan:
    def __init__(self, rows, cols, depth, edge):
        half = edge // 2
        self.rows, self.cols, self.depth, self.edge, self.half = rows, cols, depth, edge, half
        self.row_whole = rows + edge
        self.col_whole = cols + edge
        self.modes = depth // 2 + 1
        self.mode_pad = up16(self.modes)
        self.mode_step = -(-self.modes // ROWS) * ROWS
        modes = np.arange(self.modes)

        cosine, sine = waves(modes, np.arange(depth), depth)
        table = np.zeros((up16(2 * self.mode_step), depth))
        table[: self.modes] = cosine
        table[self.mode_step : self.mode_step + self.modes] = -sine
        self.depth_out = thrice(table, 1)
        weight = np.where((modes == 0) | (2 * modes == depth), 1.0, 2.0)
        weight = weight / (depth * self.row_whole * self.col_whole)
        table = np.zeros((self.mode_pad, 2 * depth))
        table[: self.modes, :depth] = cosine * weight[:, None]
        table[: self.modes, depth:] = -sine * weight[:, None]
        self.depth_home = thrice(table, 0)

        freq = np.arange(self.row_whole)
        own = self.lane_table(*self.out_waves(np.arange(rows), freq), HALF, LANES)
        place = np.concatenate([np.arange(rows, rows + half), np.arange(-half, 0)])
        halo = self.lane_table(*self.out_waves(place, freq), HALF, LANES)
        self.rows_out = thrice(np.concatenate([own, halo]), 0)
        cosine, sine = waves(freq, np.arange(rows), self.row_whole)
        self.rows_home = thrice(self.lane_table(cosine, sine, LANES, rows), 0)
        offset = np.arange(edge) - half
        self.rows_psf = thrice(self.lane_table(*self.out_waves(offset, freq), LANES, LANES), 0)

        freq = np.arange(self.col_whole)
        place = np.concatenate([np.arange(cols + half), np.arange(-half, 0)])
        self.cols_out = thrice(np.concatenate(waves(freq, place, self.col_whole)), 1)
        self.cols_home = thrice(np.concatenate(waves(np.arange(cols), freq, self.col_whole)), 1)
        self.cols_psf = thrice(np.concatenate(waves(freq, offset, self.col_whole)), 1)

    def out_waves(self, place, freq):
        cosine, sine = waves(place, freq, self.row_whole)
        return cosine, -sine

    @staticmethod
    def lane_table(real_part, imag_part, left, right):
        table = np.zeros((2 * left, 2 * right))
        height, width = real_part.shape
        table[:height, :width] = real_part
        table[:height, right : right + width] = imag_part
        table[left : left + height, :width] = -imag_part
        table[left : left + height, right : right + width] = real_part
        return table


def whole_spec(array):
    return pl.BlockSpec(array.shape, lambda i: (0,) * array.ndim)


def params():
    return pltpu.CompilerParams(
        dimension_semantics=("arbitrary",), vmem_limit_bytes=VMEM_LIMIT
    )


def cost(flops, moved):
    return pl.CostEstimate(flops=int(flops), bytes_accessed=int(moved), transcendentals=0)


def beside():
    return cost(1e6, 1e5)


def depth_out_kernel(plan, count, *refs):
    pieces, table_ref, out_ref = refs[:count], refs[count], refs[count + 1]
    sizes = [piece.shape[0] for piece in pieces]
    pieces = [piece.reshape(piece.shape[0] * ROWS, plan.depth) for piece in pieces]
    out = out_ref.reshape(plan.modes * ROWS, LANES)
    size = sum(sizes)
    group = min(ROWS, 2 * LANES // size)
    depth = plan.depth
    across = ((1,), (1,))
    for first in range(0, ROWS, group):
        slabs = [
            piece[pl.ds(j, length, stride=ROWS), :]
            for j in range(first, first + group)
            for piece, length in zip(pieces, sizes)
        ]
        high, low = split(jnp.concatenate(slabs, 0))
        result = dot(table_ref[:, : 2 * depth], jnp.concatenate([high, low], 1), across)
        result = result + dot(table_ref[:, 2 * depth :], high, across)
        real_part = result[: plan.modes]
        imag_part = result[plan.mode_step : plan.mode_step + plan.modes]
        gap = [jnp.zeros((plan.modes, HALF - size), jnp.float32)] if size < HALF else []
        for j in range(group):
            lanes = slice(j * size, (j + 1) * size)
            value = jnp.concatenate([real_part[:, lanes], *gap, imag_part[:, lanes], *gap], 1)
            out[pl.ds(first + j, plan.modes, stride=ROWS), :] = value


def depth_out(plan, name, *pieces):
    cols = pieces[0].shape[1]
    return pl.pallas_call(
        functools.partial(depth_out_kernel, plan, len(pieces)),
        grid=(cols // ROWS,),
        in_specs=[
            pl.BlockSpec((piece.shape[0], ROWS, plan.depth), lambda i: (0, i, 0))
            for piece in pieces
        ]
        + [whole_spec(plan.depth_out)],
        out_specs=pl.BlockSpec((plan.modes, ROWS, LANES), lambda i: (0, i, 0)),
        out_shape=jax.ShapeDtypeStruct((plan.modes, cols, LANES), jnp.float32),
        compiler_params=params(),
        cost_estimate=beside(),
        name=name,
    )(*pieces, plan.depth_out)


def turned_narrow(table, planes):
    both = table_by(table, jnp.concatenate(planes, 1) if len(planes) > 1 else planes[0])
    half = both.shape[0] // 2
    lane = lax.broadcasted_iota(jnp.int32, (half, LANES), 1)
    out = []
    for j in range(len(planes)):
        cosine = both[:half, j * LANES : (j + 1) * LANES]
        sine = pltpu.roll(both[half:, j * LANES : (j + 1) * LANES], HALF, 1)
        out.append(cosine + jnp.where(lane < HALF, sine, -sine))
    return out


def pairs_of(count):
    return [range(j, min(j + 2, count)) for j in range(0, count, 2)]


def cols_kernel(inner_ref, outer_ref, table_ref, out_ref):
    for pair in pairs_of(out_ref.shape[0]):
        planes = [jnp.concatenate([inner_ref[j], outer_ref[j]], 0) for j in pair]
        for j, plane in zip(pair, turned_narrow(table_ref[...], planes)):
            out_ref[j] = plane


def cols_out(plan, inner, outer):
    step = step_of(plan.modes, 13)

    def spec(size):
        return pl.BlockSpec((step, size, LANES), lambda i: (i, 0, 0))

    return pl.pallas_call(
        cols_kernel,
        grid=(plan.modes // step,),
        in_specs=[spec(plan.cols), spec(plan.edge), whole_spec(plan.cols_out)],
        out_specs=spec(plan.col_whole),
        out_shape=jax.ShapeDtypeStruct((plan.modes, plan.col_whole, LANES), jnp.float32),
        compiler_params=params(),
        cost_estimate=beside(),
        name="cols_out",
    )(inner, outer, plan.cols_out)


def turned(table, value, forward):
    both = table_by(table, value)
    half = both.shape[0] // 2
    cos_real, cos_imag = both[:half, :LANES], both[:half, LANES:]
    sin_real, sin_imag = both[half:, :LANES], both[half:, LANES:]
    if forward:
        return cos_real + sin_imag, cos_imag - sin_real
    return cos_real - sin_imag, cos_imag + sin_real


def transfer_kernel(psf_ref, rows_ref, cols_ref, out_ref):
    step, edge = psf_ref.shape[:2]
    values = by_table(jnp.concatenate([psf_ref[j] for j in range(step)], 0), rows_ref[...])
    for j in range(step):
        value = values[j * edge : (j + 1) * edge]
        out_ref[j] = jnp.concatenate(turned(cols_ref[...], value, True), 1)


def step_of(modes, most):
    return max(size for size in range(1, most + 1) if modes % size == 0)


def transfer(plan, psf):
    edge = plan.edge
    offset = np.arange(edge) - plan.half
    cosine, sine = waves(offset, np.arange(plan.modes), plan.depth)
    parts = [
        jnp.einsum(
            "abc,ck->kba",
            psf,
            jnp.asarray(table, jnp.float32),
            precision=lax.Precision.HIGHEST,
        )
        for table in (cosine, -sine)
    ]
    parts = [jnp.pad(part, ((0, 0), (0, 0), (0, LANES - edge))) for part in parts]
    modes = jnp.concatenate(parts, 2)
    step = step_of(plan.modes, 5)
    return pl.pallas_call(
        transfer_kernel,
        grid=(plan.modes // step,),
        in_specs=[
            pl.BlockSpec((step, edge, 2 * LANES), lambda i: (i, 0, 0)),
            whole_spec(plan.rows_psf),
            whole_spec(plan.cols_psf),
        ],
        out_specs=pl.BlockSpec((step, plan.col_whole, 2 * LANES), lambda i: (i, 0, 0)),
        out_shape=jax.ShapeDtypeStruct((plan.modes, plan.col_whole, 2 * LANES), jnp.float32),
        compiler_params=params(),
        cost_estimate=beside(),
        name="transfer",
    )(modes, plan.rows_psf, plan.cols_psf)


def filter_kernel(
    adjoint, own_ref, inner_ref, outer_ref, transfer_ref,
    rows_out, cols_out, cols_home, rows_home, out_ref,
):
    step, size, _ = own_ref.shape
    cols = out_ref.shape[1]
    slabs = []
    for pair in pairs_of(step):
        planes = [jnp.concatenate([inner_ref[j], outer_ref[j]], 0) for j in pair]
        for j, plane in zip(pair, turned_narrow(cols_out[...], planes)):
            slabs.append(jnp.concatenate([own_ref[j], plane], 1))
    values = by_table(jnp.concatenate(slabs, 0), rows_out[...])
    home = []
    for j in range(step):
        real_part = values[j * size : (j + 1) * size, :LANES]
        imag_part = values[j * size : (j + 1) * size, LANES:]
        gain_real = transfer_ref[j, :, :LANES]
        gain_imag = transfer_ref[j, :, LANES:]
        if adjoint:
            gain_imag = -gain_imag
        value = jnp.concatenate(
            [
                real_part * gain_real - imag_part * gain_imag,
                real_part * gain_imag + imag_part * gain_real,
            ],
            1,
        )
        home.append(jnp.concatenate(turned(cols_home[...], value, False), 1))
    values = by_table(jnp.concatenate(home, 0), rows_home[...])
    for j in range(step):
        out_ref[j] = values[j * cols : (j + 1) * cols]


def filtered(plan, own, inner, outer, gains, adjoint):
    step = step_of(plan.modes, 5)
    block = pl.BlockSpec((step, plan.col_whole, 2 * LANES), lambda i: (i, 0, 0))

    def spec(size):
        return pl.BlockSpec((step, size, LANES), lambda i: (i, 0, 0))

    tables = [plan.rows_out, plan.cols_out, plan.cols_home, plan.rows_home]
    return pl.pallas_call(
        functools.partial(filter_kernel, adjoint),
        grid=(plan.modes // step,),
        in_specs=[spec(plan.col_whole), spec(plan.cols), spec(plan.edge), block]
        + [whole_spec(table) for table in tables],
        out_specs=pl.BlockSpec((step, plan.cols, 2 * plan.rows), lambda i: (i, 0, 0)),
        out_shape=jax.ShapeDtypeStruct((plan.modes, plan.cols, 2 * plan.rows), jnp.float32),
        compiler_params=params(),
        cost_estimate=cost(2.2e10, 2.5e7),
        name="filtered",
    )(own, inner, outer, gains, *tables)


def depth_home_kernel(plan, divide, modes_ref, other_ref, table_ref, out_ref):
    lanes = 2 * plan.rows
    modes = modes_ref.reshape(plan.modes * ROWS, lanes)
    others = other_ref.reshape(plan.rows * ROWS, plan.depth)
    out = out_ref.reshape(plan.rows * ROWS, plan.depth)
    pad = jnp.zeros((plan.mode_pad - plan.modes, lanes), jnp.float32)
    for j in range(ROWS):
        slab = modes[pl.ds(j, plan.modes, stride=ROWS), :]
        high, low = split(jnp.concatenate([slab, pad], 0))
        slab = jnp.concatenate([high, low, high], 0)
        both = dot(slab, table_ref[...], ((0,), (0,)))
        result = both[: plan.rows, : plan.depth] + both[plan.rows :, plan.depth :]
        other = others[pl.ds(j, plan.rows, stride=ROWS), :]
        out[pl.ds(j, plan.rows, stride=ROWS), :] = other / result if divide else other * result


def depth_home(plan, modes, other, divide):
    block = pl.BlockSpec((plan.rows, ROWS, plan.depth), lambda i: (0, i, 0))
    return pl.pallas_call(
        functools.partial(depth_home_kernel, plan, divide),
        grid=(plan.cols // ROWS,),
        in_specs=[
            pl.BlockSpec((plan.modes, ROWS, 2 * plan.rows), lambda i: (0, i, 0)),
            block,
            whole_spec(plan.depth_home),
        ],
        out_specs=block,
        out_shape=jax.ShapeDtypeStruct((plan.rows, plan.cols, plan.depth), jnp.float32),
        compiler_params=params(),
        cost_estimate=cost(3e9, 1.3e7),
        name="depth_home",
    )(modes, other, plan.depth_home)


def neighbours(axis, after, before):
    count = lax.axis_size(axis)
    return (
        lax.ppermute(after, axis, [((i + 1) % count, i) for i in range(count)]),
        lax.ppermute(before, axis, [(i, (i + 1) % count) for i in range(count)]),
    )


def halos(block, width):
    rows = neighbours("px", block[:width], block[-width:])
    cols = jnp.concatenate(neighbours("py", block[:, :width], block[:, -width:]), 1)
    corners = neighbours("px", cols[:width], cols[-width:])
    return rows, cols, corners


def convolved(plan, block, around, gains, adjoint):
    rows, cols, corners = around
    own = cols_out(
        plan, depth_out(plan, "depth_own", block), depth_out(plan, "depth_cols", cols)
    )
    inner = depth_out(plan, "depth_rows", *rows)
    outer = depth_out(plan, "depth_corners", *corners)
    return filtered(plan, own, inner, outer, gains, adjoint)


def variation_kernel(whole, volume_ref, out_ref):
    step, cols, depth = out_ref.shape
    size = volume_ref.shape[1]
    row_start = pl.program_id(0) * step
    row_first = lax.axis_index("px") * (whole[0] // lax.axis_size("px")) + row_start - 1
    col_first = lax.axis_index("py") * cols
    sub = lax.broadcasted_iota(jnp.int32, (size, depth), 0)
    lane = lax.broadcasted_iota(jnp.int32, (size, depth), 1)
    col = col_first + jnp.where(sub <= cols, sub, sub - size)
    col_valid = (col >= 0) & (col <= whole[1] - 2)
    here = volume_ref[row_start]
    before = None
    for r in range(step + 1):
        after = volume_ref[row_start + r + 1]
        row = row_first + r
        row_valid = ((row >= 0) & (row <= whole[0] - 2)).astype(jnp.float32)
        slope_rows = (after - here) * row_valid
        slope_cols = jnp.where(col_valid, pltpu.roll(here, size - 1, 0) - here, 0.0)
        slope_depth = jnp.where(lane < depth - 1, pltpu.roll(here, depth - 1, 1) - here, 0.0)
        factor = lax.rsqrt(
            slope_rows * slope_rows
            + slope_cols * slope_cols
            + slope_depth * slope_depth
            + smoothing * smoothing
        )
        flux_rows = slope_rows * factor
        if r > 0:
            flux_cols = slope_cols * factor
            flux_depth = slope_depth * factor
            divergence = (
                (flux_rows - before)
                + (flux_cols - pltpu.roll(flux_cols, 1, 0))
                + (flux_depth - jnp.where(lane > 0, pltpu.roll(flux_depth, 1, 1), 0.0))
            )
            out_ref[r - 1] = (here / (1.0 - penalty_weight * divergence))[:cols]
        before = flux_rows
        here = after


def weighted(block, around):
    rows, cols, corners = around
    stack = [
        jnp.concatenate([corners[1][-1:], rows[1][-1:]], 1),
        jnp.concatenate([cols, block], 1),
        jnp.concatenate([corners[0][:1], rows[0][:1]], 1),
    ]
    edge, size = cols.shape[1], block.shape[1]
    volume = jnp.concatenate(
        [
            jnp.concatenate(
                [part[:, edge:], part[:, :1], part[:, edge - ROWS + 1 : edge]], 1
            )
            for part in stack
        ],
        0,
    )
    whole = (block.shape[0] * lax.axis_size("px"), size * lax.axis_size("py"))
    step = ROWS
    return pl.pallas_call(
        functools.partial(variation_kernel, whole),
        grid=(block.shape[0] // step,),
        in_specs=[whole_spec(volume)],
        out_specs=pl.BlockSpec((step,) + block.shape[1:], lambda i: (i, 0, 0)),
        out_shape=jax.ShapeDtypeStruct(block.shape, jnp.float32),
        compiler_params=params(),
        cost_estimate=beside(),
        name="weighted",
    )(volume)


def shards(estimate, observed, psf):
    rows, cols, depth = estimate.shape
    plan = Plan(rows, cols, depth, psf.shape[0])
    around = halos(estimate, plan.half)
    gains = transfer(plan, psf)
    modes = convolved(plan, estimate, around, gains, False)
    quotient = depth_home(plan, modes, observed, True)
    quotient_around = halos(quotient, plan.half)
    weight = weighted(estimate, around)
    modes = convolved(plan, quotient, quotient_around, gains, True)
    return depth_home(plan, modes, weight, False)


def solution(mesh):
    placed = (P("px", "py", None), P("px", "py", None), P())
    return jax.shard_map(
        shards, mesh=mesh, in_specs=placed, out_specs=P("px", "py", None), check_vma=False
    )
```

```python
import functools
import math

import jax
import jax.numpy as jnp
import ml_dtypes
import numpy as np
from jax import lax
from jax.experimental import pallas as pl
from jax.experimental.pallas import tpu as pltpu
from jax.sharding import PartitionSpec as P

penalty_weight = 0.1
smoothing = 0.1

LANES = 128
HALF = LANES // 2
ROWS = 8
VMEM_LIMIT = 48 * 1024 * 1024


def halves(table):
    table = np.asarray(table, np.float64).astype(np.float32)
    high = table.astype(ml_dtypes.bfloat16)
    low = (table - high.astype(np.float32)).astype(ml_dtypes.bfloat16)
    return high, low


def thrice(table, axis):
    high, low = halves(table)
    return np.concatenate([high, high, low], axis)


def waves(left, right, length):
    turns = np.remainder(np.outer(left, right), length) * (2.0 * math.pi / length)
    return np.cos(turns), np.sin(turns)


def up16(count):
    return -(-count // 16) * 16


def split(value):
    high = value.astype(jnp.bfloat16)
    low = (value - high.astype(jnp.float32)).astype(jnp.bfloat16)
    return high, low


def dot(left, right, dims=((1,), (0,))):
    return lax.dot_general(left, right, (dims, ((), ())), preferred_element_type=jnp.float32)


def by_table(value, table):
    high, low = split(value)
    return dot(jnp.concatenate([high, low, high], 1), table)


def table_by(table, value):
    high, low = split(value)
    return dot(table, jnp.concatenate([high, low, high], 0))


class Plan:
    def __init__(self, rows, cols, depth, edge):
        half = edge // 2
        self.rows, self.cols, self.depth, self.edge, self.half = rows, cols, depth, edge, half
        self.row_whole = rows + edge
        self.col_whole = cols + edge
        self.modes = depth // 2 + 1
        self.mode_pad = up16(self.modes)
        self.mode_step = -(-self.modes // ROWS) * ROWS
        modes = np.arange(self.modes)

        cosine, sine = waves(modes, np.arange(depth), depth)
        table = np.zeros((up16(2 * self.mode_step), depth))
        table[: self.modes] = cosine
        table[self.mode_step : self.mode_step + self.modes] = -sine
        self.depth_out = thrice(table, 1)
        weight = np.where((modes == 0) | (2 * modes == depth), 1.0, 2.0)
        weight = weight / (depth * self.row_whole * self.col_whole)
        table = np.zeros((self.mode_pad, 2 * depth))
        table[: self.modes, :depth] = cosine * weight[:, None]
        table[: self.modes, depth:] = -sine * weight[:, None]
        self.depth_home = thrice(table, 0)

        freq = np.arange(self.row_whole)
        own = self.lane_table(*self.out_waves(np.arange(rows), freq), HALF, LANES)
        place = np.concatenate([np.arange(rows, rows + half), np.arange(-half, 0)])
        halo = self.lane_table(*self.out_waves(place, freq), HALF, LANES)
        self.rows_out = thrice(np.concatenate([own, halo]), 0)
        cosine, sine = waves(freq, np.arange(rows), self.row_whole)
        self.rows_home = thrice(self.lane_table(cosine, sine, LANES, rows), 0)
        offset = np.arange(edge) - half
        self.rows_psf = thrice(self.lane_table(*self.out_waves(offset, freq), LANES, LANES), 0)

        freq = np.arange(self.col_whole)
        place = np.concatenate([np.arange(cols + half), np.arange(-half, 0)])
        self.cols_out = thrice(np.concatenate(waves(freq, place, self.col_whole)), 1)
        self.cols_home = thrice(np.concatenate(waves(np.arange(cols), freq, self.col_whole)), 1)
        self.cols_psf = thrice(np.concatenate(waves(freq, offset, self.col_whole)), 1)

    def out_waves(self, place, freq):
        cosine, sine = waves(place, freq, self.row_whole)
        return cosine, -sine

    @staticmethod
    def lane_table(real_part, imag_part, left, right):
        table = np.zeros((2 * left, 2 * right))
        height, width = real_part.shape
        table[:height, :width] = real_part
        table[:height, right : right + width] = imag_part
        table[left : left + height, :width] = -imag_part
        table[left : left + height, right : right + width] = real_part
        return table


def whole_spec(array):
    return pl.BlockSpec(array.shape, lambda i: (0,) * array.ndim)


def params():
    return pltpu.CompilerParams(
        dimension_semantics=("arbitrary",), vmem_limit_bytes=VMEM_LIMIT
    )


def cost(flops, moved):
    return pl.CostEstimate(flops=int(flops), bytes_accessed=int(moved), transcendentals=0)


def beside():
    return cost(1e6, 1e5)


def depth_out_kernel(plan, count, *refs):
    pieces, table_ref, out_ref = refs[:count], refs[count], refs[count + 1]
    sizes = [piece.shape[0] for piece in pieces]
    pieces = [piece.reshape(piece.shape[0] * ROWS, plan.depth) for piece in pieces]
    out = out_ref.reshape(plan.modes * ROWS, LANES)
    size = sum(sizes)
    group = min(ROWS, 2 * LANES // size)
    depth = plan.depth
    across = ((1,), (1,))
    for first in range(0, ROWS, group):
        slabs = [
            piece[pl.ds(j, length, stride=ROWS), :]
            for j in range(first, first + group)
            for piece, length in zip(pieces, sizes)
        ]
        high, low = split(jnp.concatenate(slabs, 0))
        result = dot(table_ref[:, : 2 * depth], jnp.concatenate([high, low], 1), across)
        result = result + dot(table_ref[:, 2 * depth :], high, across)
        real_part = result[: plan.modes]
        imag_part = result[plan.mode_step : plan.mode_step + plan.modes]
        gap = [jnp.zeros((plan.modes, HALF - size), jnp.float32)] if size < HALF else []
        for j in range(group):
            lanes = slice(j * size, (j + 1) * size)
            value = jnp.concatenate([real_part[:, lanes], *gap, imag_part[:, lanes], *gap], 1)
            out[pl.ds(first + j, plan.modes, stride=ROWS), :] = value


def depth_out(plan, name, *pieces):
    cols = pieces[0].shape[1]
    return pl.pallas_call(
        functools.partial(depth_out_kernel, plan, len(pieces)),
        grid=(cols // ROWS,),
        in_specs=[
            pl.BlockSpec((piece.shape[0], ROWS, plan.depth), lambda i: (0, i, 0))
            for piece in pieces
        ]
        + [whole_spec(plan.depth_out)],
        out_specs=pl.BlockSpec((plan.modes, ROWS, LANES), lambda i: (0, i, 0)),
        out_shape=jax.ShapeDtypeStruct((plan.modes, cols, LANES), jnp.float32),
        compiler_params=params(),
        cost_estimate=beside(),
        name=name,
    )(*pieces, plan.depth_out)


def turned_narrow(table, planes):
    both = table_by(table, jnp.concatenate(planes, 1) if len(planes) > 1 else planes[0])
    half = both.shape[0] // 2
    lane = lax.broadcasted_iota(jnp.int32, (half, LANES), 1)
    out = []
    for j in range(len(planes)):
        cosine = both[:half, j * LANES : (j + 1) * LANES]
        sine = pltpu.roll(both[half:, j * LANES : (j + 1) * LANES], HALF, 1)
        out.append(cosine + jnp.where(lane < HALF, sine, -sine))
    return out


def pairs_of(count):
    return [range(j, min(j + 2, count)) for j in range(0, count, 2)]


def cols_kernel(inner_ref, outer_ref, table_ref, out_ref):
    for pair in pairs_of(out_ref.shape[0]):
        planes = [jnp.concatenate([inner_ref[j], outer_ref[j]], 0) for j in pair]
        for j, plane in zip(pair, turned_narrow(table_ref[...], planes)):
            out_ref[j] = plane


def cols_out(plan, inner, outer):
    step = step_of(plan.modes, 13)

    def spec(size):
        return pl.BlockSpec((step, size, LANES), lambda i: (i, 0, 0))

    return pl.pallas_call(
        cols_kernel,
        grid=(plan.modes // step,),
        in_specs=[spec(plan.cols), spec(plan.edge), whole_spec(plan.cols_out)],
        out_specs=spec(plan.col_whole),
        out_shape=jax.ShapeDtypeStruct((plan.modes, plan.col_whole, LANES), jnp.float32),
        compiler_params=params(),
        cost_estimate=beside(),
        name="cols_out",
    )(inner, outer, plan.cols_out)


def turned(table, value, forward):
    both = table_by(table, value)
    half = both.shape[0] // 2
    cos_real, cos_imag = both[:half, :LANES], both[:half, LANES:]
    sin_real, sin_imag = both[half:, :LANES], both[half:, LANES:]
    if forward:
        return cos_real + sin_imag, cos_imag - sin_real
    return cos_real - sin_imag, cos_imag + sin_real


def transfer_kernel(psf_ref, rows_ref, cols_ref, out_ref):
    step, edge = psf_ref.shape[:2]
    values = by_table(jnp.concatenate([psf_ref[j] for j in range(step)], 0), rows_ref[...])
    for j in range(step):
        value = values[j * edge : (j + 1) * edge]
        out_ref[j] = jnp.concatenate(turned(cols_ref[...], value, True), 1)


def step_of(modes, most):
    return max(size for size in range(1, most + 1) if modes % size == 0)


def transfer(plan, psf):
    edge = plan.edge
    offset = np.arange(edge) - plan.half
    cosine, sine = waves(offset, np.arange(plan.modes), plan.depth)
    parts = [
        jnp.einsum(
            "abc,ck->kba",
            psf,
            jnp.asarray(table, jnp.float32),
            precision=lax.Precision.HIGHEST,
        )
        for table in (cosine, -sine)
    ]
    parts = [jnp.pad(part, ((0, 0), (0, 0), (0, LANES - edge))) for part in parts]
    modes = jnp.concatenate(parts, 2)
    step = step_of(plan.modes, 5)
    return pl.pallas_call(
        transfer_kernel,
        grid=(plan.modes // step,),
        in_specs=[
            pl.BlockSpec((step, edge, 2 * LANES), lambda i: (i, 0, 0)),
            whole_spec(plan.rows_psf),
            whole_spec(plan.cols_psf),
        ],
        out_specs=pl.BlockSpec((step, plan.col_whole, 2 * LANES), lambda i: (i, 0, 0)),
        out_shape=jax.ShapeDtypeStruct((plan.modes, plan.col_whole, 2 * LANES), jnp.float32),
        compiler_params=params(),
        cost_estimate=beside(),
        name="transfer",
    )(modes, plan.rows_psf, plan.cols_psf)


def filter_kernel(
    adjoint, own_ref, inner_ref, outer_ref, transfer_ref,
    rows_out, cols_out, cols_home, rows_home, out_ref,
):
    step, size, _ = own_ref.shape
    cols = out_ref.shape[1]
    slabs = []
    for pair in pairs_of(step):
        planes = [jnp.concatenate([inner_ref[j], outer_ref[j]], 0) for j in pair]
        for j, plane in zip(pair, turned_narrow(cols_out[...], planes)):
            slabs.append(jnp.concatenate([own_ref[j], plane], 1))
    values = by_table(jnp.concatenate(slabs, 0), rows_out[...])
    home = []
    for j in range(step):
        real_part = values[j * size : (j + 1) * size, :LANES]
        imag_part = values[j * size : (j + 1) * size, LANES:]
        gain_real = transfer_ref[j, :, :LANES]
        gain_imag = transfer_ref[j, :, LANES:]
        if adjoint:
            gain_imag = -gain_imag
        value = jnp.concatenate(
            [
                real_part * gain_real - imag_part * gain_imag,
                real_part * gain_imag + imag_part * gain_real,
            ],
            1,
        )
        home.append(jnp.concatenate(turned(cols_home[...], value, False), 1))
    values = by_table(jnp.concatenate(home, 0), rows_home[...])
    for j in range(step):
        out_ref[j] = values[j * cols : (j + 1) * cols]


def filtered(plan, own, inner, outer, gains, adjoint):
    step = step_of(plan.modes, 5)
    block = pl.BlockSpec((step, plan.col_whole, 2 * LANES), lambda i: (i, 0, 0))

    def spec(size):
        return pl.BlockSpec((step, size, LANES), lambda i: (i, 0, 0))

    tables = [plan.rows_out, plan.cols_out, plan.cols_home, plan.rows_home]
    return pl.pallas_call(
        functools.partial(filter_kernel, adjoint),
        grid=(plan.modes // step,),
        in_specs=[spec(plan.col_whole), spec(plan.cols), spec(plan.edge), block]
        + [whole_spec(table) for table in tables],
        out_specs=pl.BlockSpec((step, plan.cols, 2 * plan.rows), lambda i: (i, 0, 0)),
        out_shape=jax.ShapeDtypeStruct((plan.modes, plan.cols, 2 * plan.rows), jnp.float32),
        compiler_params=params(),
        cost_estimate=cost(2.2e10, 2.5e7),
        name="filtered",
    )(own, inner, outer, gains, *tables)


def depth_home_kernel(plan, divide, modes_ref, other_ref, table_ref, out_ref):
    lanes = 2 * plan.rows
    modes = modes_ref.reshape(plan.modes * ROWS, lanes)
    others = other_ref.reshape(plan.rows * ROWS, plan.depth)
    out = out_ref.reshape(plan.rows * ROWS, plan.depth)
    pad = jnp.zeros((plan.mode_pad - plan.modes, lanes), jnp.float32)
    for j in range(ROWS):
        slab = modes[pl.ds(j, plan.modes, stride=ROWS), :]
        high, low = split(jnp.concatenate([slab, pad], 0))
        slab = jnp.concatenate([high, low, high], 0)
        both = dot(slab, table_ref[...], ((0,), (0,)))
        result = both[: plan.rows, : plan.depth] + both[plan.rows :, plan.depth :]
        other = others[pl.ds(j, plan.rows, stride=ROWS), :]
        out[pl.ds(j, plan.rows, stride=ROWS), :] = other / result if divide else other * result


def depth_home(plan, modes, other, divide):
    block = pl.BlockSpec((plan.rows, ROWS, plan.depth), lambda i: (0, i, 0))
    return pl.pallas_call(
        functools.partial(depth_home_kernel, plan, divide),
        grid=(plan.cols // ROWS,),
        in_specs=[
            pl.BlockSpec((plan.modes, ROWS, 2 * plan.rows), lambda i: (0, i, 0)),
            block,
            whole_spec(plan.depth_home),
        ],
        out_specs=block,
        out_shape=jax.ShapeDtypeStruct((plan.rows, plan.cols, plan.depth), jnp.float32),
        compiler_params=params(),
        cost_estimate=cost(3e9, 1.3e7),
        name="depth_home",
    )(modes, other, plan.depth_home)


def neighbours(axis, after, before):
    count = lax.axis_size(axis)
    return (
        lax.ppermute(after, axis, [((i + 1) % count, i) for i in range(count)]),
        lax.ppermute(before, axis, [(i, (i + 1) % count) for i in range(count)]),
    )


def halos(block, width):
    rows = neighbours("px", block[:width], block[-width:])
    cols = jnp.concatenate(neighbours("py", block[:, :width], block[:, -width:]), 1)
    first = jnp.concatenate([part[:, :width] for part in rows], 0)
    last = jnp.concatenate([part[:, -width:] for part in rows], 0)
    corners = jnp.concatenate(neighbours("py", first, last), 1)
    return rows, cols, corners


def convolved(plan, block, around, gains, adjoint):
    rows, cols, corners = around
    own = cols_out(
        plan, depth_out(plan, "depth_own", block), depth_out(plan, "depth_cols", cols)
    )
    inner = depth_out(plan, "depth_rows", *rows)
    outer = depth_out(plan, "depth_corners", corners)
    return filtered(plan, own, inner, outer, gains, adjoint)


def variation_kernel(whole, volume_ref, out_ref):
    step, cols, depth = out_ref.shape
    size = volume_ref.shape[1]
    row_start = pl.program_id(0) * step
    row_first = lax.axis_index("px") * (whole[0] // lax.axis_size("px")) + row_start - 1
    col_first = lax.axis_index("py") * cols
    sub = lax.broadcasted_iota(jnp.int32, (size, depth), 0)
    lane = lax.broadcasted_iota(jnp.int32, (size, depth), 1)
    col = col_first + jnp.where(sub <= cols, sub, sub - size)
    col_valid = (col >= 0) & (col <= whole[1] - 2)
    here = volume_ref[row_start]
    before = None
    for r in range(step + 1):
        after = volume_ref[row_start + r + 1]
        row = row_first + r
        row_valid = ((row >= 0) & (row <= whole[0] - 2)).astype(jnp.float32)
        slope_rows = (after - here) * row_valid
        slope_cols = jnp.where(col_valid, pltpu.roll(here, size - 1, 0) - here, 0.0)
        slope_depth = jnp.where(lane < depth - 1, pltpu.roll(here, depth - 1, 1) - here, 0.0)
        factor = lax.rsqrt(
            slope_rows * slope_rows
            + slope_cols * slope_cols
            + slope_depth * slope_depth
            + smoothing * smoothing
        )
        flux_rows = slope_rows * factor
        if r > 0:
            flux_cols = slope_cols * factor
            flux_depth = slope_depth * factor
            divergence = (
                (flux_rows - before)
                + (flux_cols - pltpu.roll(flux_cols, 1, 0))
                + (flux_depth - jnp.where(lane > 0, pltpu.roll(flux_depth, 1, 1), 0.0))
            )
            out_ref[r - 1] = (here / (1.0 - penalty_weight * divergence))[:cols]
        before = flux_rows
        here = after


def weighted(block, around):
    rows, cols, corners = around
    stack = [
        jnp.concatenate([corners[-1:], rows[1][-1:]], 1),
        jnp.concatenate([cols, block], 1),
        jnp.concatenate([corners[:1], rows[0][:1]], 1),
    ]
    edge, size = cols.shape[1], block.shape[1]
    volume = jnp.concatenate(
        [
            jnp.concatenate(
                [part[:, edge:], part[:, :1], part[:, edge - ROWS + 1 : edge]], 1
            )
            for part in stack
        ],
        0,
    )
    whole = (block.shape[0] * lax.axis_size("px"), size * lax.axis_size("py"))
    step = ROWS
    return pl.pallas_call(
        functools.partial(variation_kernel, whole),
        grid=(block.shape[0] // step,),
        in_specs=[whole_spec(volume)],
        out_specs=pl.BlockSpec((step,) + block.shape[1:], lambda i: (i, 0, 0)),
        out_shape=jax.ShapeDtypeStruct(block.shape, jnp.float32),
        compiler_params=params(),
        cost_estimate=beside(),
        name="weighted",
    )(volume)


def shards(estimate, observed, psf):
    rows, cols, depth = estimate.shape
    plan = Plan(rows, cols, depth, psf.shape[0])
    around = halos(estimate, plan.half)
    gains = transfer(plan, psf)
    modes = convolved(plan, estimate, around, gains, False)
    quotient = depth_home(plan, modes, observed, True)
    quotient_around = halos(quotient, plan.half)
    weight = weighted(estimate, around)
    modes = convolved(plan, quotient, quotient_around, gains, True)
    return depth_home(plan, modes, weight, False)


def solution(mesh):
    placed = (P("px", "py", None), P("px", "py", None), P())
    return jax.shard_map(
        shards, mesh=mesh, in_specs=placed, out_specs=P("px", "py", None), check_vma=False
    )
```

```python
import functools
import math

import jax
import jax.numpy as jnp
import ml_dtypes
import numpy as np
from jax import lax
from jax.experimental import pallas as pl
from jax.experimental.pallas import tpu as pltpu
from jax.sharding import PartitionSpec as P

penalty_weight = 0.1
smoothing = 0.1

LANES = 128
HALF = LANES // 2
ROWS = 8
VMEM_LIMIT = 48 * 1024 * 1024


def halves(table):
    table = np.asarray(table, np.float64).astype(np.float32)
    high = table.astype(ml_dtypes.bfloat16)
    low = (table - high.astype(np.float32)).astype(ml_dtypes.bfloat16)
    return high, low


def thrice(table, axis):
    high, low = halves(table)
    return np.concatenate([high, high, low], axis)


def waves(left, right, length):
    turns = np.remainder(np.outer(left, right), length) * (2.0 * math.pi / length)
    return np.cos(turns), np.sin(turns)


def up16(count):
    return -(-count // 16) * 16


def split(value):
    high = value.astype(jnp.bfloat16)
    low = (value - high.astype(jnp.float32)).astype(jnp.bfloat16)
    return high, low


def dot(left, right, dims=((1,), (0,))):
    return lax.dot_general(left, right, (dims, ((), ())), preferred_element_type=jnp.float32)


def by_table(value, table):
    high, low = split(value)
    return dot(jnp.concatenate([high, low, high], 1), table)


def table_by(table, value):
    high, low = split(value)
    return dot(table, jnp.concatenate([high, low, high], 0))


class Plan:
    def __init__(self, rows, cols, depth, edge):
        half = edge // 2
        self.rows, self.cols, self.depth, self.edge, self.half = rows, cols, depth, edge, half
        self.row_whole = rows + edge
        self.col_whole = cols + edge
        self.modes = depth // 2 + 1
        self.mode_pad = up16(self.modes)
        self.mode_step = -(-self.modes // ROWS) * ROWS
        modes = np.arange(self.modes)

        cosine, sine = waves(modes, np.arange(depth), depth)
        table = np.zeros((up16(2 * self.mode_step), depth))
        table[: self.modes] = cosine
        table[self.mode_step : self.mode_step + self.modes] = -sine
        self.depth_out = thrice(table, 1)
        weight = np.where((modes == 0) | (2 * modes == depth), 1.0, 2.0)
        weight = weight / (depth * self.row_whole * self.col_whole)
        table = np.zeros((self.mode_pad, 2 * depth))
        table[: self.modes, :depth] = cosine * weight[:, None]
        table[: self.modes, depth:] = -sine * weight[:, None]
        self.depth_home = thrice(table, 0)

        freq = np.arange(self.row_whole)
        own = self.lane_table(*self.out_waves(np.arange(rows), freq), HALF, LANES)
        place = np.concatenate([np.arange(rows, rows + half), np.arange(-half, 0)])
        halo = self.lane_table(*self.out_waves(place, freq), HALF, LANES)
        self.rows_out = thrice(np.concatenate([own, halo]), 0)
        cosine, sine = waves(freq, np.arange(rows), self.row_whole)
        self.rows_home = thrice(self.lane_table(cosine, sine, LANES, rows), 0)
        offset = np.arange(edge) - half
        self.rows_psf = thrice(self.lane_table(*self.out_waves(offset, freq), LANES, LANES), 0)

        freq = np.arange(self.col_whole)
        place = np.concatenate([np.arange(cols + half), np.arange(-half, 0)])
        self.cols_out = thrice(np.concatenate(waves(freq, place, self.col_whole)), 1)
        self.cols_home = thrice(np.concatenate(waves(np.arange(cols), freq, self.col_whole)), 1)
        self.cols_psf = thrice(np.concatenate(waves(freq, offset, self.col_whole)), 1)

    def out_waves(self, place, freq):
        cosine, sine = waves(place, freq, self.row_whole)
        return cosine, -sine

    @staticmethod
    def lane_table(real_part, imag_part, left, right):
        table = np.zeros((2 * left, 2 * right))
        height, width = real_part.shape
        table[:height, :width] = real_part
        table[:height, right : right + width] = imag_part
        table[left : left + height, :width] = -imag_part
        table[left : left + height, right : right + width] = real_part
        return table


def whole_spec(array):
    return pl.BlockSpec(array.shape, lambda i: (0,) * array.ndim)


def params():
    return pltpu.CompilerParams(
        dimension_semantics=("arbitrary",), vmem_limit_bytes=VMEM_LIMIT
    )


def cost(flops, moved):
    return pl.CostEstimate(flops=int(flops), bytes_accessed=int(moved), transcendentals=0)


def beside():
    return cost(1e6, 1e5)


def depth_out_kernel(plan, count, *refs):
    pieces, table_ref, out_ref = refs[:count], refs[count], refs[count + 1]
    sizes = [piece.shape[0] for piece in pieces]
    pieces = [piece.reshape(piece.shape[0] * ROWS, plan.depth) for piece in pieces]
    out = out_ref.reshape(plan.modes * ROWS, LANES)
    size = sum(sizes)
    group = min(ROWS, 2 * LANES // size)
    depth = plan.depth
    across = ((1,), (1,))
    for first in range(0, ROWS, group):
        slabs = [
            piece[pl.ds(j, length, stride=ROWS), :]
            for j in range(first, first + group)
            for piece, length in zip(pieces, sizes)
        ]
        high, low = split(jnp.concatenate(slabs, 0))
        result = dot(table_ref[:, : 2 * depth], jnp.concatenate([high, low], 1), across)
        result = result + dot(table_ref[:, 2 * depth :], high, across)
        real_part = result[: plan.modes]
        imag_part = result[plan.mode_step : plan.mode_step + plan.modes]
        gap = [jnp.zeros((plan.modes, HALF - size), jnp.float32)] if size < HALF else []
        for j in range(group):
            lanes = slice(j * size, (j + 1) * size)
            value = jnp.concatenate([real_part[:, lanes], *gap, imag_part[:, lanes], *gap], 1)
            out[pl.ds(first + j, plan.modes, stride=ROWS), :] = value


def depth_out(plan, name, *pieces):
    cols = pieces[0].shape[1]
    return pl.pallas_call(
        functools.partial(depth_out_kernel, plan, len(pieces)),
        grid=(cols // ROWS,),
        in_specs=[
            pl.BlockSpec((piece.shape[0], ROWS, plan.depth), lambda i: (0, i, 0))
            for piece in pieces
        ]
        + [whole_spec(plan.depth_out)],
        out_specs=pl.BlockSpec((plan.modes, ROWS, LANES), lambda i: (0, i, 0)),
        out_shape=jax.ShapeDtypeStruct((plan.modes, cols, LANES), jnp.float32),
        compiler_params=params(),
        cost_estimate=beside(),
        name=name,
    )(*pieces, plan.depth_out)


def turned_narrow(table, planes):
    both = table_by(table, jnp.concatenate(planes, 1) if len(planes) > 1 else planes[0])
    half = both.shape[0] // 2
    lane = lax.broadcasted_iota(jnp.int32, (half, LANES), 1)
    out = []
    for j in range(len(planes)):
        cosine = both[:half, j * LANES : (j + 1) * LANES]
        sine = pltpu.roll(both[half:, j * LANES : (j + 1) * LANES], HALF, 1)
        out.append(cosine + jnp.where(lane < HALF, sine, -sine))
    return out


def pairs_of(count):
    return [range(j, min(j + 2, count)) for j in range(0, count, 2)]


def cols_kernel(inner_ref, outer_ref, table_ref, out_ref):
    for pair in pairs_of(out_ref.shape[0]):
        planes = [jnp.concatenate([inner_ref[j], outer_ref[j]], 0) for j in pair]
        for j, plane in zip(pair, turned_narrow(table_ref[...], planes)):
            out_ref[j] = plane


def cols_out(plan, inner, outer):
    step = step_of(plan.modes, 13)

    def spec(size):
        return pl.BlockSpec((step, size, LANES), lambda i: (i, 0, 0))

    return pl.pallas_call(
        cols_kernel,
        grid=(plan.modes // step,),
        in_specs=[spec(plan.cols), spec(plan.edge), whole_spec(plan.cols_out)],
        out_specs=spec(plan.col_whole),
        out_shape=jax.ShapeDtypeStruct((plan.modes, plan.col_whole, LANES), jnp.float32),
        compiler_params=params(),
        cost_estimate=beside(),
        name="cols_out",
    )(inner, outer, plan.cols_out)


def turned(table, value, forward):
    both = table_by(table, value)
    half = both.shape[0] // 2
    cos_real, cos_imag = both[:half, :LANES], both[:half, LANES:]
    sin_real, sin_imag = both[half:, :LANES], both[half:, LANES:]
    if forward:
        return cos_real + sin_imag, cos_imag - sin_real
    return cos_real - sin_imag, cos_imag + sin_real


def transfer_kernel(psf_ref, rows_ref, cols_ref, out_ref):
    step, edge = psf_ref.shape[:2]
    values = by_table(jnp.concatenate([psf_ref[j] for j in range(step)], 0), rows_ref[...])
    for j in range(step):
        value = values[j * edge : (j + 1) * edge]
        out_ref[j] = jnp.concatenate(turned(cols_ref[...], value, True), 1)


def step_of(modes, most):
    return max(size for size in range(1, most + 1) if modes % size == 0)


def transfer(plan, psf):
    edge = plan.edge
    offset = np.arange(edge) - plan.half
    cosine, sine = waves(offset, np.arange(plan.modes), plan.depth)
    parts = [
        jnp.einsum(
            "abc,ck->kba",
            psf,
            jnp.asarray(table, jnp.float32),
            precision=lax.Precision.HIGHEST,
        )
        for table in (cosine, -sine)
    ]
    parts = [jnp.pad(part, ((0, 0), (0, 0), (0, LANES - edge))) for part in parts]
    modes = jnp.concatenate(parts, 2)
    step = step_of(plan.modes, 5)
    return pl.pallas_call(
        transfer_kernel,
        grid=(plan.modes // step,),
        in_specs=[
            pl.BlockSpec((step, edge, 2 * LANES), lambda i: (i, 0, 0)),
            whole_spec(plan.rows_psf),
            whole_spec(plan.cols_psf),
        ],
        out_specs=pl.BlockSpec((step, plan.col_whole, 2 * LANES), lambda i: (i, 0, 0)),
        out_shape=jax.ShapeDtypeStruct((plan.modes, plan.col_whole, 2 * LANES), jnp.float32),
        compiler_params=params(),
        cost_estimate=beside(),
        name="transfer",
    )(modes, plan.rows_psf, plan.cols_psf)


def filter_kernel(
    adjoint, own_ref, inner_ref, outer_ref, transfer_ref,
    rows_out, cols_out, cols_home, rows_home, out_ref,
):
    step, size, _ = own_ref.shape
    cols = out_ref.shape[1]
    slabs = []
    for pair in pairs_of(step):
        planes = [jnp.concatenate([inner_ref[j], outer_ref[j]], 0) for j in pair]
        for j, plane in zip(pair, turned_narrow(cols_out[...], planes)):
            slabs.append(jnp.concatenate([own_ref[j], plane], 1))
    values = by_table(jnp.concatenate(slabs, 0), rows_out[...])
    home = []
    for j in range(step):
        real_part = values[j * size : (j + 1) * size, :LANES]
        imag_part = values[j * size : (j + 1) * size, LANES:]
        gain_real = transfer_ref[j, :, :LANES]
        gain_imag = transfer_ref[j, :, LANES:]
        if adjoint:
            gain_imag = -gain_imag
        value = jnp.concatenate(
            [
                real_part * gain_real - imag_part * gain_imag,
                real_part * gain_imag + imag_part * gain_real,
            ],
            1,
        )
        home.append(jnp.concatenate(turned(cols_home[...], value, False), 1))
    values = by_table(jnp.concatenate(home, 0), rows_home[...])
    for j in range(step):
        out_ref[j] = values[j * cols : (j + 1) * cols]


def filtered(plan, own, inner, outer, gains, adjoint):
    step = step_of(plan.modes, 5)
    block = pl.BlockSpec((step, plan.col_whole, 2 * LANES), lambda i: (i, 0, 0))

    def spec(size):
        return pl.BlockSpec((step, size, LANES), lambda i: (i, 0, 0))

    tables = [plan.rows_out, plan.cols_out, plan.cols_home, plan.rows_home]
    return pl.pallas_call(
        functools.partial(filter_kernel, adjoint),
        grid=(plan.modes // step,),
        in_specs=[spec(plan.col_whole), spec(plan.cols), spec(plan.edge), block]
        + [whole_spec(table) for table in tables],
        out_specs=pl.BlockSpec((step, plan.cols, 2 * plan.rows), lambda i: (i, 0, 0)),
        out_shape=jax.ShapeDtypeStruct((plan.modes, plan.cols, 2 * plan.rows), jnp.float32),
        compiler_params=params(),
        cost_estimate=cost(2.2e10, 2.5e7),
        name="filtered",
    )(own, inner, outer, gains, *tables)


def depth_home_kernel(plan, divide, modes_ref, other_ref, table_ref, out_ref):
    lanes = 2 * plan.rows
    modes = modes_ref.reshape(plan.modes * ROWS, lanes)
    others = other_ref.reshape(plan.rows * ROWS, plan.depth)
    out = out_ref.reshape(plan.rows * ROWS, plan.depth)
    pad = jnp.zeros((plan.mode_pad - plan.modes, lanes), jnp.float32)
    for j in range(ROWS):
        slab = modes[pl.ds(j, plan.modes, stride=ROWS), :]
        high, low = split(jnp.concatenate([slab, pad], 0))
        slab = jnp.concatenate([high, low, high], 0)
        both = dot(slab, table_ref[...], ((0,), (0,)))
        result = both[: plan.rows, : plan.depth] + both[plan.rows :, plan.depth :]
        other = others[pl.ds(j, plan.rows, stride=ROWS), :]
        out[pl.ds(j, plan.rows, stride=ROWS), :] = other / result if divide else other * result


def depth_home(plan, modes, other, divide):
    block = pl.BlockSpec((plan.rows, ROWS, plan.depth), lambda i: (0, i, 0))
    return pl.pallas_call(
        functools.partial(depth_home_kernel, plan, divide),
        grid=(plan.cols // ROWS,),
        in_specs=[
            pl.BlockSpec((plan.modes, ROWS, 2 * plan.rows), lambda i: (0, i, 0)),
            block,
            whole_spec(plan.depth_home),
        ],
        out_specs=block,
        out_shape=jax.ShapeDtypeStruct((plan.rows, plan.cols, plan.depth), jnp.float32),
        compiler_params=params(),
        cost_estimate=cost(3e9, 1.3e7),
        name="depth_home",
    )(modes, other, plan.depth_home)


def neighbours(axis, after, before):
    count = lax.axis_size(axis)
    return (
        lax.ppermute(after, axis, [((i + 1) % count, i) for i in range(count)]),
        lax.ppermute(before, axis, [(i, (i + 1) % count) for i in range(count)]),
    )


def convolved(plan, block, gains, adjoint, beside_rows):
    width = plan.half
    rows = neighbours("px", block[:width], block[-width:])
    cols = jnp.concatenate(neighbours("py", block[:, :width], block[:, -width:]), 1)
    own = cols_out(
        plan, depth_out(plan, "depth_own", block), depth_out(plan, "depth_cols", cols)
    )
    rows, own, beside_rows = lax.optimization_barrier((rows, own, beside_rows))
    first = jnp.concatenate([part[:, :width] for part in rows], 0)
    last = jnp.concatenate([part[:, -width:] for part in rows], 0)
    corners = jnp.concatenate(neighbours("py", first, last), 1)
    inner = depth_out(plan, "depth_rows", *rows)
    outer = depth_out(plan, "depth_corners", corners)
    if gains is None:
        gains = beside_rows
    modes = filtered(plan, own, inner, outer, gains, adjoint)
    return modes, (rows, cols, corners), beside_rows


def variation_kernel(whole, volume_ref, out_ref):
    step, cols, depth = out_ref.shape
    size = volume_ref.shape[1]
    row_start = pl.program_id(0) * step
    row_first = lax.axis_index("px") * (whole[0] // lax.axis_size("px")) + row_start - 1
    col_first = lax.axis_index("py") * cols
    sub = lax.broadcasted_iota(jnp.int32, (size, depth), 0)
    lane = lax.broadcasted_iota(jnp.int32, (size, depth), 1)
    col = col_first + jnp.where(sub <= cols, sub, sub - size)
    col_valid = (col >= 0) & (col <= whole[1] - 2)
    here = volume_ref[row_start]
    before = None
    for r in range(step + 1):
        after = volume_ref[row_start + r + 1]
        row = row_first + r
        row_valid = ((row >= 0) & (row <= whole[0] - 2)).astype(jnp.float32)
        slope_rows = (after - here) * row_valid
        slope_cols = jnp.where(col_valid, pltpu.roll(here, size - 1, 0) - here, 0.0)
        slope_depth = jnp.where(lane < depth - 1, pltpu.roll(here, depth - 1, 1) - here, 0.0)
        factor = lax.rsqrt(
            slope_rows * slope_rows
            + slope_cols * slope_cols
            + slope_depth * slope_depth
            + smoothing * smoothing
        )
        flux_rows = slope_rows * factor
        if r > 0:
            flux_cols = slope_cols * factor
            flux_depth = slope_depth * factor
            divergence = (
                (flux_rows - before)
                + (flux_cols - pltpu.roll(flux_cols, 1, 0))
                + (flux_depth - jnp.where(lane > 0, pltpu.roll(flux_depth, 1, 1), 0.0))
            )
            out_ref[r - 1] = (here / (1.0 - penalty_weight * divergence))[:cols]
        before = flux_rows
        here = after


def weighted(block, around):
    rows, cols, corners = around
    stack = [
        jnp.concatenate([corners[-1:], rows[1][-1:]], 1),
        jnp.concatenate([cols, block], 1),
        jnp.concatenate([corners[:1], rows[0][:1]], 1),
    ]
    edge, size = cols.shape[1], block.shape[1]
    volume = jnp.concatenate(
        [
            jnp.concatenate(
                [part[:, edge:], part[:, :1], part[:, edge - ROWS + 1 : edge]], 1
            )
            for part in stack
        ],
        0,
    )
    whole = (block.shape[0] * lax.axis_size("px"), size * lax.axis_size("py"))
    step = ROWS
    return pl.pallas_call(
        functools.partial(variation_kernel, whole),
        grid=(block.shape[0] // step,),
        in_specs=[whole_spec(volume)],
        out_specs=pl.BlockSpec((step,) + block.shape[1:], lambda i: (i, 0, 0)),
        out_shape=jax.ShapeDtypeStruct(block.shape, jnp.float32),
        compiler_params=params(),
        cost_estimate=beside(),
        name="weighted",
    )(volume)


def shards(estimate, observed, psf):
    rows, cols, depth = estimate.shape
    plan = Plan(rows, cols, depth, psf.shape[0])
    modes, around, gains = convolved(plan, estimate, None, False, transfer(plan, psf))
    quotient = depth_home(plan, modes, observed, True)
    weight = weighted(estimate, around)
    modes, _, weight = convolved(plan, quotient, gains, True, weight)
    return depth_home(plan, modes, weight, False)


def solution(mesh):
    placed = (P("px", "py", None), P("px", "py", None), P())
    return jax.shard_map(
        shards, mesh=mesh, in_specs=placed, out_specs=P("px", "py", None), check_vma=False
    )
```
